512 devices in a mesh: graph: 64 (over y, z_lo, core), fsdp: 8 (over z_hi, x).
Axes of the slice: x: 4, y: 8, z: 8 (z_hi: 2, z_lo: 4; z = z_hi * 4 + z_lo), core: 2. Of those that a mesh axis runs over, the one named last changes fastest.
Arguments:
- node_features: bfloat16 [8, 8192, 512], P('fsdp', 'graph'), may hold values from -6 to 6
- out_grad: bfloat16 [8, 8192, 512], P('fsdp', 'graph'), may hold values from -6 to 6
- send_weight: bfloat16 [2, 512, 512], P(None, 'fsdp'), may hold values from -0.25 to 0.25
- recv_weight: bfloat16 [2, 512, 512], P(None, 'fsdp'), may hold values from -0.25 to 0.25
- gain: float32 [2, 512], replicated, may hold values from 0.1 to 1.9
- senders: int32 [64, 512], P('graph'), may hold values from 0 to 143, as said below
- receivers: int32 [64, 512], P('graph'), may hold values from 0 to 127
- edge_count: int32 [64], P('graph'), may hold values from 256 to 512, as said below
- send_rows: int32 [64, 2, 8], P('graph'), may hold values from 0 to 127, as said below
Outputs:
- updated: bfloat16 [8, 8192, 512], P('fsdp', 'graph')
- feature_grad: bfloat16 [8, 8192, 512], P('fsdp', 'graph')
- send_grad: float32 [2, 512, 512], P(None, 'fsdp')
- recv_grad: float32 [2, 512, 512], P(None, 'fsdp')
- gain_grad: float32 [2, 512], replicated
The draws below stay inside these ranges and needn't reach their ends.
Inputs may be any that keep to these rules, and one draw needn't show every extreme that they name: `senders`: rows 0 to 127 are the partition's own, the next 8 came from the previous partition, the last 8 from the next. The live slots of a partition are its first edge_count slots; some partition fills all 512. `send_rows`: the 16 rows of one partition are distinct.
All inputs are finite; a program needn't handle non-finite values.
Results may differ from the reference program's by a relative error of at most 0.019.
Values may be sent and summed in bfloat16 or wider, within the bound.
No kernel may reach another device: no remote copies, remote signals or barrier semaphores. Data moves between devices by JAX's collectives and lax.ppermute only.
A program may use at most 64 MiB of HBM per device.

```python
import jax
import jax.numpy as jnp
from jax import lax

D = 512
LAYERS = 2
NODE_DEV = 128
HALO = 8
EDGE_CAP = 512
NODES = 8192
N_GRAPH = 64
N_FSDP = 8


def draw_senders(key, part):
    key = jax.random.fold_in(key, 5)
    first, second, third, fourth = jax.random.split(key, 4)
    picks = jax.random.randint(first, (N_GRAPH, EDGE_CAP), 0, 8, dtype=jnp.int32)
    own_ids = jax.random.randint(second, (N_GRAPH, EDGE_CAP), 0, NODE_DEV, dtype=jnp.int32)
    halo_ids = jax.random.randint(third, (N_GRAPH, EDGE_CAP), NODE_DEV, NODE_DEV + 2 * HALO, dtype=jnp.int32)
    values = jnp.where(picks == 0, halo_ids, own_ids)
    chosen = jax.random.randint(fourth, (), 0, N_GRAPH, dtype=jnp.int32)
    values = values.at[chosen, 0].set(NODE_DEV + 2 * HALO - 1)
    return values.at[chosen, 1].set(0)


def draw_receivers(key, part):
    key = jax.random.fold_in(key, 7)
    first, second = jax.random.split(key)
    values = jax.random.randint(first, (N_GRAPH, EDGE_CAP), 0, NODE_DEV, dtype=jnp.int32)
    chosen = jax.random.randint(second, (), 0, N_GRAPH, dtype=jnp.int32)
    values = values.at[chosen, 0].set(NODE_DEV - 1)
    return values.at[chosen, 1].set(0)


def draw_edge_count(key, part):
    key = jax.random.fold_in(key, 9)
    first, second, third = jax.random.split(key, 3)
    counts = jax.random.randint(first, (N_GRAPH,), EDGE_CAP // 2, EDGE_CAP + 1, dtype=jnp.int32)
    fullest = jax.random.randint(second, (), 0, N_GRAPH, dtype=jnp.int32)
    emptiest = jax.random.randint(third, (), 0, N_GRAPH, dtype=jnp.int32)
    counts = counts.at[emptiest].set(EDGE_CAP // 2)
    return counts.at[fullest].set(EDGE_CAP)


def draw_send_rows(key, part):
    key = jax.random.fold_in(key, 13)
    keys = jax.random.split(key, N_GRAPH)
    orders = jax.vmap(lambda single: jax.random.permutation(single, NODE_DEV)[:2 * HALO])(keys)
    return orders.astype(jnp.int32).reshape(N_GRAPH, 2, HALO)


def level_of(key, shape, cuts, least, high):
    def one(position, blocks):
        draws = jax.random.uniform(jax.random.fold_in(jax.random.fold_in(key, 6), position), (blocks,), jnp.float32, least / len(cuts), high / len(cuts))
        return jnp.repeat(jnp.exp(draws), shape[position] // blocks).reshape((-1,) + (1,) * (len(shape) - position - 1))

    factor_of = one(*cuts[0])
    for cut in cuts[1:]:
        factor_of = factor_of * one(*cut)
    return factor_of


def scatter_about(own_key, shape, scale, limit, shards=(), kind=jnp.bfloat16):
    drawn = jax.random.normal(own_key, shape, jnp.float32) * scale
    if len(shards) > 0:
        drawn = level_of(own_key, shape, shards, -0.22, 0.18) * drawn
    return jnp.clip(drawn, min=-limit, max=limit).astype(kind)


def setup_inputs(seed: int = 0) -> dict:
    key_list = jax.random.split(jax.random.key(seed), 10)
    return {
        "node_features": scatter_about(key_list[0], (N_FSDP, NODES, D), 1.0, 6.0, ((0, 8), (1, 64))),
        "out_grad": scatter_about(key_list[1], (N_FSDP, NODES, D), 1.0, 6.0, ((0, 8), (1, 64))),
        "send_weight": scatter_about(key_list[2], (LAYERS, D, D), D ** -0.5, 0.25, ((1, 8),)),
        "recv_weight": scatter_about(key_list[3], (LAYERS, D, D), D ** -0.5, 0.25, ((1, 8),)),
        "gain": jnp.clip(1.0 + 0.18 * jax.random.normal(key_list[4], (LAYERS, D), jnp.float32), 0.1, 1.9),
        "senders": draw_senders(jax.random.fold_in(key_list[9], 71), 0),
        "receivers": draw_receivers(jax.random.fold_in(key_list[9], 71), 0),
        "edge_count": draw_edge_count(jax.random.fold_in(key_list[9], 71), 0),
        "send_rows": draw_send_rows(jax.random.fold_in(key_list[9], 71), 0),
    }


EPSILON = 1e-05
loss_scale = 512.0

def layer_local(ext_rows, own_rows, send_matrix, recv_matrix, gain_row, sender_ids, receiver_ids, live_mask):
    proj_send = jnp.dot(ext_rows, send_matrix, preferred_element_type=jnp.float32)
    proj_recv = jnp.dot(own_rows, recv_matrix, preferred_element_type=jnp.float32)
    preact = jnp.take(proj_send, sender_ids, axis=0) + jnp.take(proj_recv, receiver_ids, axis=0)
    message = jax.nn.silu(preact) * live_mask[:, None]
    total = jax.ops.segment_sum(message, receiver_ids, num_segments=own_rows.shape[0])
    factor = lax.rsqrt(lax.optimization_barrier(jnp.mean(total * total, axis=-1, keepdims=True)) + EPSILON)
    return (own_rows.astype(jnp.float32) + gain_row[None, :] * total * factor).astype(jnp.bfloat16)

def pullback_of(ext_rows, own_rows, send_matrix, recv_matrix, gain_row, sender_ids, receiver_ids, live_mask):

    def local_map(ext_in, own_in, send_in, recv_in, gain_in):
        return layer_local(ext_in, own_in, send_in, recv_in, gain_in, sender_ids, receiver_ids, live_mask)
    return jax.vjp(local_map, ext_rows, own_rows, send_matrix, recv_matrix, gain_row)

def local_grads(ext_rows, own_rows, send_matrix, recv_matrix, gain_row, sender_ids, receiver_ids, live_mask, cotangent):
    result, pullback = pullback_of(ext_rows, own_rows, send_matrix, recv_matrix, gain_row, sender_ids, receiver_ids, live_mask)
    return pullback(cotangent)

def reference(node_features, out_grad, send_weight, recv_weight, gain, senders, receivers, edge_count, send_rows):
    layer_total = send_weight.shape[0]
    own_count = NODE_DEV
    halo_count = HALO
    partitions = senders.shape[0]
    live_mask = (jnp.arange(EDGE_CAP, dtype=jnp.int32)[None, :] < edge_count[:, None]).astype(jnp.float32)
    upper_ids = send_rows[:, 0]
    lower_ids = send_rows[:, 1]
    pick_rows = jax.vmap(lambda source, index_rows: jnp.take(source, index_rows, axis=0))
    add_rows = jax.vmap(lambda target, first_ids, second_ids, first_rows, second_rows: target.at[first_ids].add(first_rows).at[second_ids].add(second_rows))
    run_layer = jax.vmap(layer_local, in_axes=(0, 0, None, None, None, 0, 0, 0))
    run_grads = jax.vmap(local_grads, in_axes=(0, 0, None, None, None, 0, 0, 0, 0))

    def extend(blocks):
        from_prev = jnp.roll(pick_rows(blocks, upper_ids), 1, axis=0)
        from_next = jnp.roll(pick_rows(blocks, lower_ids), -1, axis=0)
        return jnp.concatenate([blocks, from_prev, from_next], axis=1)

    def one_sample(sample_pair):
        sample_rows, sample_grad = sample_pair
        blocks = sample_rows.reshape(partitions, own_count, sample_rows.shape[1])
        stored = []
        for layer_index in range(layer_total):
            ext_rows = extend(blocks)
            stored.append((ext_rows, blocks))
            blocks = run_layer(ext_rows, blocks, send_weight[layer_index], recv_weight[layer_index], gain[layer_index], senders, receivers, live_mask)
        cotangent = sample_grad.reshape(partitions, own_count, sample_grad.shape[1])
        send_sums = [None] * layer_total
        recv_sums = [None] * layer_total
        gain_sums = [None] * layer_total
        for layer_index in reversed(range(layer_total)):
            ext_rows, own_rows = stored[layer_index]
            ext_grad, own_grad, send_term, recv_term, gain_term = run_grads(ext_rows, own_rows, send_weight[layer_index], recv_weight[layer_index], gain[layer_index], senders, receivers, live_mask, cotangent)
            send_sums[layer_index] = lax.optimization_barrier(jnp.sum(send_term.astype(jnp.float32), axis=0))
            recv_sums[layer_index] = lax.optimization_barrier(jnp.sum(recv_term.astype(jnp.float32), axis=0))
            gain_sums[layer_index] = lax.optimization_barrier(jnp.sum(gain_term, axis=0))
            back_up = jnp.roll(ext_grad[:, own_count:own_count + halo_count], -1, axis=0)
            back_down = jnp.roll(ext_grad[:, own_count + halo_count:], 1, axis=0)
            merged = own_grad.astype(jnp.float32) + ext_grad[:, :own_count].astype(jnp.float32)
            merged = add_rows(merged, upper_ids, lower_ids, back_up.astype(jnp.float32), back_down.astype(jnp.float32))
            cotangent = merged.astype(jnp.bfloat16)
        width = blocks.shape[2]
        return (blocks.reshape(partitions * own_count, width), cotangent.reshape(partitions * own_count, width), jnp.stack(send_sums), jnp.stack(recv_sums), jnp.stack(gain_sums))
    updated, feature_grad, send_all, recv_all, gain_all = lax.map(one_sample, (node_features, out_grad))
    return (updated, feature_grad, lax.optimization_barrier(jnp.sum(send_all, axis=0)) / loss_scale, lax.optimization_barrier(jnp.sum(recv_all, axis=0)) / loss_scale, lax.optimization_barrier(jnp.sum(gain_all, axis=0)) / loss_scale)
```

```python
import functools

import jax
import jax.numpy as jnp
from jax import lax
from jax.experimental import pallas as pl
from jax.experimental.pallas import tpu as pltpu
from jax.sharding import Mesh
from jax.sharding import PartitionSpec as P

EPSILON = 1e-05
LOSS_SCALE = 512.0

D = 512
N = 128
H = 16
E = 512
EXT = N + 2 * H
ROWS = EXT + N
HALF = D // 2
DROWS = ROWS + 16
CHUNK_LANES = 4 * HALF + 128

BF = jnp.bfloat16
F32 = jnp.float32
VMEM = pl.BlockSpec(memory_space=pltpu.VMEM)
SMEM = pl.BlockSpec(memory_space=pltpu.SMEM)


def dot(a, b):
    return jnp.dot(a, b, preferred_element_type=F32)


def dot_tn(a, b):
    return lax.dot_general(a, b, (((0,), (0,)), ((), ())), preferred_element_type=F32)


def dot_nt(a, b):
    return lax.dot_general(a, b, (((1,), (1,)), ((), ())), preferred_element_type=F32)


def split(value):
    high = value.astype(BF)
    return high, (value - high.astype(F32)).astype(BF)


def call(kernel, outs, name, *args, flops=1e8):
    specs = [SMEM if a.dtype == jnp.int32 and a.size <= 2 else VMEM for a in args]
    return pl.pallas_call(
        kernel,
        out_shape=[jax.ShapeDtypeStruct(s, t) for s, t in outs],
        in_specs=specs,
        out_specs=[VMEM] * len(outs),
        compiler_params=pltpu.CompilerParams(vmem_limit_bytes=40 * 1024 * 1024),
        cost_estimate=pl.CostEstimate(flops=int(flops), bytes_accessed=2000000, transcendentals=0),
        name=name,
    )(*args)


def send_matrix_of(send_rows_ref):
    rows = lax.broadcasted_iota(jnp.int32, (N, H), 0)
    return (rows == send_rows_ref[...]).astype(F32).astype(BF)


def prepare_kernel(count, senders, receivers, send_rows, rows, by_row, by_edge, sent):
    live = lax.broadcasted_iota(jnp.int32, (1, E), 1) < count[0, 0]
    ids = senders[...]
    ids = jnp.where(ids >= N + H // 2, ids + H, ids)
    ids = jnp.where(live, ids, -1)
    receiver_ids = jnp.where(live, receivers[...], -1)
    row = lax.broadcasted_iota(jnp.int32, (EXT, E), 0)
    by_row[0:EXT, :] = (row == ids).astype(F32).astype(BF)
    row = lax.broadcasted_iota(jnp.int32, (N, E), 0)
    by_row[EXT:ROWS, :] = (row == receiver_ids).astype(F32).astype(BF)
    ids_down = jnp.broadcast_to(ids, (N, E)).T
    receivers_down = jnp.broadcast_to(receiver_ids, (N, E)).T
    lane = lax.broadcasted_iota(jnp.int32, (E, N), 1)
    by_edge[0] = (lane == ids_down).astype(F32).astype(BF)
    by_edge[1] = (lane == receivers_down).astype(F32).astype(BF)
    by_edge[2] = (lane == ids_down - N).astype(F32).astype(BF)
    sent[...] = dot_tn(send_matrix_of(send_rows), rows[...]).astype(BF)


def weights_of(core, own, peer):
    def whole(ref):
        return jnp.concatenate([ref[x, z] for z in range(2) for x in range(4)], axis=0)

    first, second = whole(own), whole(peer)
    is_first = core[0, 0] == 0
    return jnp.where(is_first, first, second), jnp.where(is_first, second, first)


def forward(rows, from_prev, from_next, send_matrix, recv_matrix, by_row, by_edge):
    ext = jnp.concatenate([rows, from_prev, from_next], axis=0)
    proj_send = dot(ext, send_matrix)
    proj_recv = dot(rows, recv_matrix)
    send_high, send_low = split(proj_send)
    recv_high, recv_low = split(proj_recv)
    halo = jnp.concatenate(
        [send_high[N:], send_low[N:], jnp.zeros((N - 4 * H, D), BF)], axis=0
    )
    halo_edges = by_edge[2]
    halo_edges = jnp.concatenate(
        [halo_edges[:, : 2 * H], halo_edges[:, : 2 * H], halo_edges[:, 4 * H :]], axis=1
    )
    edges = jnp.concatenate([by_edge[0], by_edge[1]], axis=1)
    own_high = jnp.concatenate([send_high[:N], recv_high], axis=0)
    own_low = jnp.concatenate([send_low[:N], recv_low], axis=0)
    preact = dot(edges, own_high) + dot(edges, own_low) + dot(halo_edges, halo)
    sigmoid = 1.0 / (1.0 + jnp.exp(-preact))
    message = preact * sigmoid
    slope = sigmoid * (1.0 + preact * (1.0 - sigmoid))
    high, low = split(message)
    receive = by_row[EXT:ROWS, :]
    return dot(receive, high) + dot(receive, low), slope


def factor_of(total):
    return lax.rsqrt(jnp.mean(total * total, axis=-1, keepdims=True) + EPSILON)


def backward(cotangent, total, slope, gain_row, send_matrix, recv_matrix, by_row, by_edge):
    factor = factor_of(total)
    normal = total * factor
    gain_term = jnp.sum(cotangent * normal, axis=0, keepdims=True)
    scaled = cotangent * gain_row
    inner = jnp.mean(scaled * normal, axis=-1, keepdims=True)
    total_grad = (scaled - normal * inner) * factor
    high, low = split(total_grad)
    receive = by_edge[1]
    preact_grad = ((dot(receive, high) + dot(receive, low)) * slope).astype(BF)
    row_grad = dot(by_row[...], preact_grad).astype(BF)
    send_rows_grad, recv_rows_grad = row_grad[:EXT], row_grad[EXT:]
    ext_grad = dot_nt(send_rows_grad, send_matrix)
    own_grad = dot_nt(recv_rows_grad, recv_matrix) + ext_grad[:N]
    halo_grad = ext_grad[N:].astype(BF)
    gain_block = jnp.concatenate([gain_term, jnp.zeros((15, D), F32)], axis=0).astype(BF)
    return own_grad, halo_grad[:H], halo_grad[H:], row_grad, gain_block


def halves(core, value):
    is_first = core[0, 0] == 0
    left, right = value[:, :HALF], value[:, HALF:]
    return jnp.where(is_first, left, right), jnp.where(is_first, right, left)


def first_layer_kernel(
    core, rows, from_prev, from_next, own, peer, gain, by_row, by_edge, send_rows,
    result, total_out, slope_out, sent,
):
    send_matrix, recv_matrix = weights_of(core, own, peer)
    total, slope = forward(
        rows[...], from_prev[...], from_next[...], send_matrix, recv_matrix, by_row, by_edge
    )
    total_out[...] = total
    slope_out[...] = slope
    new = (rows[...].astype(F32) + gain[0:1, :] * total * factor_of(total)).astype(BF)
    result[...] = new
    sent[...] = dot_tn(send_matrix_of(send_rows), new).astype(BF)


def last_layer_kernel(
    core, rows, from_prev, from_next, own, peer, gain, by_row, by_edge, out_grad,
    result, own_grad, to_prev, to_next, keep, give,
):
    send_matrix, recv_matrix = weights_of(core, own, peer)
    total, slope = forward(
        rows[...], from_prev[...], from_next[...], send_matrix, recv_matrix, by_row, by_edge
    )
    gain_row = gain[1:2, :]
    result[...] = (rows[...].astype(F32) + gain_row * total * factor_of(total)).astype(BF)
    cotangent = out_grad[...].astype(F32)
    grad, prev_grad, next_grad, row_grad, gain_block = backward(
        cotangent, total, slope, gain_row, send_matrix, recv_matrix, by_row, by_edge
    )
    own_grad[...] = grad + cotangent
    to_prev[...] = prev_grad
    to_next[...] = next_grad
    keep[0:ROWS, :], give[0:ROWS, :] = halves(core, row_grad)
    keep[ROWS:DROWS, :], give[ROWS:DROWS, :] = halves(core, gain_block)


def merged(own_grad, from_next, from_prev, send_rows):
    back = (from_next[...].astype(F32) + from_prev[...].astype(F32)).astype(BF)
    return (own_grad[...] + dot(send_matrix_of(send_rows), back)).astype(BF)


def back_kernel(
    core, later_grad, back_next, back_prev, total, slope, own, peer, gain, by_row, by_edge, send_rows,
    rows_0, prev_0, next_0, rows_1, prev_1, next_1, later_keep, later_give,
    own_grad, to_prev, to_next, keep, pack,
):
    send_matrix, recv_matrix = weights_of(core, own, peer)
    cotangent = merged(later_grad, back_next, back_prev, send_rows).astype(F32)
    grad, prev_grad, next_grad, row_grad, gain_block = backward(
        cotangent, total[...], slope[...], gain[0:1, :], send_matrix, recv_matrix, by_row, by_edge
    )
    own_grad[...] = grad + cotangent
    to_prev[...] = prev_grad
    to_next[...] = next_grad
    base = 2 * EXT
    keep_rows, give_rows = halves(core, row_grad)
    keep_gain, give_gain = halves(core, gain_block)
    keep[0:ROWS, 0:HALF] = keep_rows
    keep[ROWS:DROWS, 0:HALF] = keep_gain
    keep[:, HALF:D] = later_keep[...]
    pack[base : base + ROWS, 0:HALF] = give_rows
    pack[base + ROWS : base + DROWS, 0:HALF] = give_gain
    pack[base : base + DROWS, HALF:D] = later_give[...]
    for layer, parts in enumerate(((rows_0, prev_0, next_0), (rows_1, prev_1, next_1))):
        start = layer * EXT
        pack[start : start + N, :] = parts[0][...]
        pack[start + N : start + N + H, :] = parts[1][...]
        pack[start + N + H : start + EXT, :] = parts[2][...]


def merge_kernel(own_grad, back_next, back_prev, send_rows, result):
    result[...] = merged(own_grad, back_next, back_prev, send_rows)


def terms_kernel(pack, keep, peer, chunks):
    base = 2 * EXT
    gains = []
    for layer in range(2):
        lanes = slice(layer * HALF, (layer + 1) * HALF)
        mine = pack[layer * EXT : (layer + 1) * EXT, :]
        theirs = peer[layer * EXT : (layer + 1) * EXT, :]
        for kind in range(2):
            if kind == 0:
                left = jnp.concatenate([mine, theirs], axis=0)
                right = jnp.concatenate([keep[0:EXT, lanes], peer[base : base + EXT, lanes]], axis=0)
            else:
                left = jnp.concatenate([mine[:N], theirs[:N]], axis=0)
                right = jnp.concatenate(
                    [keep[EXT:ROWS, lanes], peer[base + EXT : base + ROWS, lanes]], axis=0
                )
            term = dot_tn(left, right).astype(BF)
            for block in range(8):
                for part in range(4):
                    start = block * 64 + part * 16
                    chunks[block, 2 * kind + layer, :, part * HALF : (part + 1) * HALF] = term[
                        start : start + 16
                    ]
        gain = keep[ROWS:DROWS, lanes].astype(F32) + peer[base + ROWS : base + DROWS, lanes].astype(F32)
        gains += [gain[0:1, :128], gain[0:1, 128:]]
    block = jnp.concatenate(gains + [jnp.zeros((12, 128), F32)], axis=0).astype(BF)
    for first in range(8):
        for second in range(4):
            chunks[first, second, :, 4 * HALF :] = block


def first_sum_kernel(parts, copies):
    total = parts[0].astype(F32)
    for source in range(1, 32):
        total = total + parts[source].astype(F32)
    total = total.astype(BF)
    for target in range(32):
        copies[target] = total


def second_sum_kernel(parts, result):
    for place in range(4):
        total = parts[place].astype(F32)
        for source in range(1, 8):
            total = total + parts[4 * source + place].astype(F32)
        result[place] = total.astype(BF)


def spread_kernel(core, own, peer, send_grad, recv_grad, gain_grad):
    is_first = core[0, 0] == 0
    scale = 1.0 / LOSS_SCALE
    mine, theirs = own[...].astype(F32) * scale, peer[...].astype(F32) * scale
    sides = (jnp.where(is_first, mine, theirs), jnp.where(is_first, theirs, mine))
    for side, value in enumerate(sides):
        for matrix in range(4):
            out = (send_grad, recv_grad)[matrix // 2]
            for part in range(4):
                out[matrix % 2, part * 16 : part * 16 + 16, side * HALF : (side + 1) * HALF] = value[
                    matrix, :, part * HALF : (part + 1) * HALF
                ]
        for layer in range(2):
            for half in range(2):
                start = side * HALF + half * 128
                row = layer * 2 + half
                gain_grad[layer : layer + 1, start : start + 128] = value[0, row : row + 1, 4 * HALF :]


GRAPH = ("y", "zl", "c")


def shift(value, steps):
    return lax.ppermute(value, GRAPH, [(i, (i + steps) % 64) for i in range(64)])


def swap(value, axis):
    return lax.ppermute(value, axis, [(0, 1), (1, 0)])


def shards(
    node_features, out_grad, send_weight, recv_weight, gain, senders, receivers, edge_count, send_rows
):
    core = lax.axis_index("c").astype(jnp.int32).reshape(1, 1)
    features = node_features[0]
    targets = send_rows.reshape(1, H)
    half = jnp.where(lax.axis_index("c") == 0, send_weight, recv_weight)
    other = swap(half, "zh")
    by_row, by_edge, sent_0 = call(
        prepare_kernel,
        [((ROWS, E), BF), ((3, E, N), BF), ((H, D), BF)],
        "prepare",
        edge_count.reshape(1, 1), senders, receivers, targets, features,
    )
    prev_0, next_0 = shift(sent_0, 1), shift(sent_0, -1)
    is_low = lax.axis_index("zh") == 0
    both = jnp.stack([jnp.where(is_low, half, other), jnp.where(is_low, other, half)], axis=1)
    copies = jnp.broadcast_to(both[None], (4,) + both.shape)
    gathered = lax.all_to_all(copies, ("x",), 0, 0, tiled=True)
    own = [gathered[:, layer] for layer in range(2)]
    peer = [swap(value, "c") for value in own]

    rows_1, total_0, slope_0, sent_1 = call(
        first_layer_kernel,
        [((N, D), BF), ((N, D), F32), ((E, D), F32), ((H, D), BF)],
        "first_layer",
        core, features, prev_0, next_0, own[0], peer[0], gain, by_row, by_edge, targets,
    )
    prev_1, next_1 = shift(sent_1, 1), shift(sent_1, -1)
    updated, grad_1, to_prev, to_next, keep_1, give_1 = call(
        last_layer_kernel,
        [((N, D), BF), ((N, D), F32), ((H, D), BF), ((H, D), BF), ((DROWS, HALF), BF), ((DROWS, HALF), BF)],
        "last_layer",
        core, rows_1, prev_1, next_1, own[1], peer[1], gain, by_row, by_edge, out_grad[0],
    )
    back_next, back_prev = shift(to_prev, -1), shift(to_next, 1)
    grad_0, to_prev, to_next, keep, pack = call(
        back_kernel,
        [((N, D), F32), ((H, D), BF), ((H, D), BF), ((DROWS, D), BF), ((2 * EXT + DROWS, D), BF)],
        "back",
        core, grad_1, back_next, back_prev, total_0, slope_0, own[0], peer[0], gain, by_row, by_edge,
        targets, features, prev_0, next_0, rows_1, prev_1, next_1, keep_1, give_1,
    )
    peer_pack = swap(pack, "c")
    back_next, back_prev = shift(to_prev, -1), shift(to_next, 1)
    (chunks,) = call(terms_kernel, [((8, 4, 16, CHUNK_LANES), BF)], "terms", pack, keep, peer_pack)
    chunks = chunks.reshape(32, 16, CHUNK_LANES)
    parts = lax.all_to_all(chunks, ("zh", "x", "zl"), 0, 0, tiled=True)
    (copies,) = call(first_sum_kernel, [((32, 16, CHUNK_LANES), BF)], "first_sum", parts)
    parts = lax.all_to_all(copies, ("y", "zl"), 0, 0, tiled=True)
    (mine,) = call(second_sum_kernel, [((4, 16, CHUNK_LANES), BF)], "second_sum", parts)
    theirs = swap(mine, "c")
    send_grad, recv_grad, gain_grad = call(
        spread_kernel, [((2, 64, D), F32), ((2, 64, D), F32), ((2, D), F32)], "spread", core, mine, theirs
    )
    (feature_grad,) = call(merge_kernel, [((N, D), BF)], "merge", grad_0, back_next, back_prev, targets)
    return updated[None], feature_grad[None], send_grad, recv_grad, gain_grad


def solution(mesh):
    graph, fsdp = GRAPH, ("zh", "x")
    wide = Mesh(mesh.devices.reshape(8, 4, 2, 2, 4), GRAPH + fsdp)
    in_specs = (
        P(fsdp, graph, None),
        P(fsdp, graph, None),
        P(None, fsdp, None),
        P(None, fsdp, None),
        P(),
        P(graph, None),
        P(graph, None),
        P(graph),
        P(graph, None, None),
    )
    out_specs = (
        P(fsdp, graph, None),
        P(fsdp, graph, None),
        P(None, fsdp, None),
        P(None, fsdp, None),
        P(),
    )
    return jax.shard_map(shards, mesh=wide, in_specs=in_specs, out_specs=out_specs, check_vma=False)
```

```python
import functools

import jax
import jax.numpy as jnp
from jax import lax
from jax.experimental import pallas as pl
from jax.experimental.pallas import tpu as pltpu
from jax.sharding import Mesh
from jax.sharding import PartitionSpec as P

EPSILON = 1e-05
LOSS_SCALE = 512.0

D = 512
N = 128
H = 16
E = 512
EXT = N + 2 * H
ROWS = EXT + N
HALF = D // 2
DROWS = ROWS + 16
PARTS = 64

BF = jnp.bfloat16
F32 = jnp.float32
VMEM = pl.BlockSpec(memory_space=pltpu.VMEM)
SMEM = pl.BlockSpec(memory_space=pltpu.SMEM)


def dot(a, b):
    return jnp.dot(a, b, preferred_element_type=F32)


def dot_tn(a, b):
    return lax.dot_general(a, b, (((0,), (0,)), ((), ())), preferred_element_type=F32)


def dot_nt(a, b):
    return lax.dot_general(a, b, (((1,), (1,)), ((), ())), preferred_element_type=F32)


def split(value):
    high = value.astype(BF)
    return high, (value - high.astype(F32)).astype(BF)


def call(kernel, outs, name, *args, flops=1e8):
    specs = [SMEM if a.dtype == jnp.int32 and a.size <= 2 else VMEM for a in args]
    return pl.pallas_call(
        kernel,
        out_shape=[jax.ShapeDtypeStruct(s, t) for s, t in outs],
        in_specs=specs,
        out_specs=[VMEM] * len(outs),
        compiler_params=pltpu.CompilerParams(vmem_limit_bytes=40 * 1024 * 1024),
        cost_estimate=pl.CostEstimate(flops=int(flops), bytes_accessed=2000000, transcendentals=0),
        name=name,
    )(*args)


def send_matrix_of(send_rows_ref):
    rows = lax.broadcasted_iota(jnp.int32, (N, H), 0)
    return (rows == send_rows_ref[...]).astype(F32).astype(BF)


def prepare_kernel(count, senders, receivers, send_rows, rows, by_row, by_edge, sent):
    live = lax.broadcasted_iota(jnp.int32, (1, E), 1) < count[0, 0]
    ids = senders[...]
    ids = jnp.where(ids >= N + H // 2, ids + H, ids)
    ids = jnp.where(live, ids, -1)
    receiver_ids = jnp.where(live, receivers[...], -1)
    row = lax.broadcasted_iota(jnp.int32, (EXT, E), 0)
    by_row[0:EXT, :] = (row == ids).astype(F32).astype(BF)
    row = lax.broadcasted_iota(jnp.int32, (N, E), 0)
    by_row[EXT:ROWS, :] = (row == receiver_ids).astype(F32).astype(BF)
    ids_down = jnp.broadcast_to(ids, (N, E)).T
    receivers_down = jnp.broadcast_to(receiver_ids, (N, E)).T
    lane = lax.broadcasted_iota(jnp.int32, (E, N), 1)
    by_edge[0] = (lane == ids_down).astype(F32).astype(BF)
    by_edge[1] = (lane == receivers_down).astype(F32).astype(BF)
    by_edge[2] = (lane == ids_down - N).astype(F32).astype(BF)
    sent[...] = dot_tn(send_matrix_of(send_rows), rows[...]).astype(BF)


def weights_of(core, own, peer, layer):
    def whole(ref):
        return jnp.concatenate([ref[x, z, layer] for z in range(2) for x in range(4)], axis=0)

    first, second = whole(own), whole(peer)
    is_first = core[0, 0] == 0
    return jnp.where(is_first, first, second), jnp.where(is_first, second, first)


def forward(rows, from_prev, from_next, send_matrix, recv_matrix, by_row, by_edge):
    ext = jnp.concatenate([rows, from_prev, from_next], axis=0)
    proj_send = dot(ext, send_matrix)
    proj_recv = dot(rows, recv_matrix)
    send_high, send_low = split(proj_send)
    recv_high, recv_low = split(proj_recv)
    halo = jnp.concatenate(
        [send_high[N:], send_low[N:], jnp.zeros((N - 4 * H, D), BF)], axis=0
    )
    halo_edges = by_edge[2]
    halo_edges = jnp.concatenate(
        [halo_edges[:, : 2 * H], halo_edges[:, : 2 * H], halo_edges[:, 4 * H :]], axis=1
    )
    edges = jnp.concatenate([by_edge[0], by_edge[1]], axis=1)
    own_high = jnp.concatenate([send_high[:N], recv_high], axis=0)
    own_low = jnp.concatenate([send_low[:N], recv_low], axis=0)
    preact = dot(edges, own_high) + dot(edges, own_low) + dot(halo_edges, halo)
    sigmoid = 1.0 / (1.0 + jnp.exp(-preact))
    message = preact * sigmoid
    slope = sigmoid * (1.0 + preact * (1.0 - sigmoid))
    high, low = split(message)
    receive = by_row[EXT:ROWS, :]
    return dot(receive, high) + dot(receive, low), slope


def factor_of(total):
    return lax.rsqrt(jnp.mean(total * total, axis=-1, keepdims=True) + EPSILON)


def backward(cotangent, total, slope, gain_row, send_matrix, recv_matrix, by_row, by_edge):
    factor = factor_of(total)
    normal = total * factor
    gain_term = jnp.sum(cotangent * normal, axis=0, keepdims=True)
    scaled = cotangent * gain_row
    inner = jnp.mean(scaled * normal, axis=-1, keepdims=True)
    total_grad = (scaled - normal * inner) * factor
    high, low = split(total_grad)
    receive = by_edge[1]
    preact_grad = ((dot(receive, high) + dot(receive, low)) * slope).astype(BF)
    row_grad = dot(by_row[...], preact_grad).astype(BF)
    send_rows_grad, recv_rows_grad = row_grad[:EXT], row_grad[EXT:]
    ext_grad = dot_nt(send_rows_grad, send_matrix)
    own_grad = dot_nt(recv_rows_grad, recv_matrix) + ext_grad[:N]
    halo_grad = ext_grad[N:].astype(BF)
    gain_block = jnp.concatenate([gain_term, jnp.zeros((15, D), F32)], axis=0).astype(BF)
    return own_grad, halo_grad[:H], halo_grad[H:], row_grad, gain_block


def halves(core, value):
    is_first = core[0, 0] == 0
    left, right = value[:, :HALF], value[:, HALF:]
    return jnp.where(is_first, left, right), jnp.where(is_first, right, left)


def first_layer_kernel(
    core, rows, from_prev, from_next, own, peer, gain, by_row, by_edge, send_rows,
    result, total_out, slope_out, sent,
):
    send_matrix, recv_matrix = weights_of(core, own, peer, 0)
    total, slope = forward(
        rows[...], from_prev[...], from_next[...], send_matrix, recv_matrix, by_row, by_edge
    )
    total_out[...] = total
    slope_out[...] = slope
    new = (rows[...].astype(F32) + gain[0:1, :] * total * factor_of(total)).astype(BF)
    result[...] = new
    sent[...] = dot_tn(send_matrix_of(send_rows), new).astype(BF)


def last_layer_kernel(
    core, rows, from_prev, from_next, own, peer, gain, by_row, by_edge, out_grad,
    result, own_grad, to_prev, to_next, keep, give,
):
    send_matrix, recv_matrix = weights_of(core, own, peer, 1)
    total, slope = forward(
        rows[...], from_prev[...], from_next[...], send_matrix, recv_matrix, by_row, by_edge
    )
    gain_row = gain[1:2, :]
    result[...] = (rows[...].astype(F32) + gain_row * total * factor_of(total)).astype(BF)
    cotangent = out_grad[...].astype(F32)
    grad, prev_grad, next_grad, row_grad, gain_block = backward(
        cotangent, total, slope, gain_row, send_matrix, recv_matrix, by_row, by_edge
    )
    own_grad[...] = grad + cotangent
    to_prev[...] = prev_grad
    to_next[...] = next_grad
    keep[0:ROWS, :], give[0:ROWS, :] = halves(core, row_grad)
    keep[ROWS:DROWS, :], give[ROWS:DROWS, :] = halves(core, gain_block)


def merged(own_grad, from_next, from_prev, send_rows):
    back = (from_next[...].astype(F32) + from_prev[...].astype(F32)).astype(BF)
    return (own_grad[...] + dot(send_matrix_of(send_rows), back)).astype(BF)


def back_kernel(
    core, later_grad, back_next, back_prev, total, slope, own, peer, gain, by_row, by_edge, send_rows,
    rows_0, prev_0, next_0, rows_1, prev_1, next_1, later_keep, later_give,
    own_grad, to_prev, to_next, keep, pack,
):
    send_matrix, recv_matrix = weights_of(core, own, peer, 0)
    cotangent = merged(later_grad, back_next, back_prev, send_rows).astype(F32)
    grad, prev_grad, next_grad, row_grad, gain_block = backward(
        cotangent, total[...], slope[...], gain[0:1, :], send_matrix, recv_matrix, by_row, by_edge
    )
    own_grad[...] = grad + cotangent
    to_prev[...] = prev_grad
    to_next[...] = next_grad
    base = 2 * EXT
    keep_rows, give_rows = halves(core, row_grad)
    keep_gain, give_gain = halves(core, gain_block)
    keep[0:ROWS, 0:HALF] = keep_rows
    keep[ROWS:DROWS, 0:HALF] = keep_gain
    keep[:, HALF:D] = later_keep[...]
    pack[base : base + ROWS, 0:HALF] = give_rows
    pack[base + ROWS : base + DROWS, 0:HALF] = give_gain
    pack[base : base + DROWS, HALF:D] = later_give[...]
    for layer, parts in enumerate(((rows_0, prev_0, next_0), (rows_1, prev_1, next_1))):
        start = layer * EXT
        pack[start : start + N, :] = parts[0][...]
        pack[start + N : start + N + H, :] = parts[1][...]
        pack[start + N + H : start + EXT, :] = parts[2][...]


def merge_kernel(own_grad, back_next, back_prev, send_rows, result):
    result[...] = merged(own_grad, back_next, back_prev, send_rows)


def terms_kernel(pack, keep, peer, chunks):
    base = 2 * EXT
    gains = []
    for layer in range(2):
        lanes = slice(layer * HALF, (layer + 1) * HALF)
        mine = pack[layer * EXT : (layer + 1) * EXT, :]
        theirs = peer[layer * EXT : (layer + 1) * EXT, :]
        for kind in range(2):
            if kind == 0:
                left = jnp.concatenate([mine, theirs], axis=0)
                right = jnp.concatenate([keep[0:EXT, lanes], peer[base : base + EXT, lanes]], axis=0)
            else:
                left = jnp.concatenate([mine[:N], theirs[:N]], axis=0)
                right = jnp.concatenate(
                    [keep[EXT:ROWS, lanes], peer[base + EXT : base + ROWS, lanes]], axis=0
                )
            term = dot_tn(left, right).astype(BF)
            for z in range(2):
                for x in range(4):
                    start = (z * 4 + x) * 64
                    place = (z * 4 + 2 * kind + layer) * 64
                    chunks[x, place : place + 64, :] = term[start : start + 64]
        gain = keep[ROWS:DROWS, lanes].astype(F32) + peer[base + ROWS : base + DROWS, lanes].astype(F32)
        gains.append(gain[0:1, :])
    block = jnp.concatenate(gains + [jnp.zeros((14, HALF), F32)], axis=0).astype(BF)
    for x in range(4):
        chunks[x, 512:528, :] = block


def first_sum_kernel(parts, pieces):
    total = parts[0].astype(F32)
    for source in range(1, 4):
        total = total + parts[source].astype(F32)
    gains = [total[512 + layer : 513 + layer, half : half + 128] for layer in range(2) for half in (0, 128)]
    gain = jnp.concatenate(gains + [jnp.zeros((4, 128), F32)], axis=0).astype(BF)
    for y in range(8):
        for z in range(8):
            start = z * 64 + y * 8
            pieces[y * 8 + z, :, 0:HALF] = total[start : start + 8].astype(BF)
            pieces[y * 8 + z, :, HALF:] = gain


def second_sum_kernel(parts, copies):
    total = parts[0].astype(F32)
    for source in range(1, PARTS):
        total = total + parts[source].astype(F32)
    total = total.astype(BF)
    for target in range(32):
        copies[target] = total


def spread_kernel(core, own, peer, send_grad, recv_grad, gain_grad):
    is_first = core[0, 0] == 0
    scale = 1.0 / LOSS_SCALE
    mine, theirs = own[...].astype(F32) * scale, peer[...].astype(F32) * scale
    sides = (jnp.where(is_first, mine, theirs), jnp.where(is_first, theirs, mine))
    for side, value in enumerate(sides):
        columns = slice(side * HALF, (side + 1) * HALF)
        for matrix in range(4):
            out = (send_grad, recv_grad)[matrix // 2]
            for y in range(8):
                out[matrix % 2, y * 8 : y * 8 + 8, columns] = value[y * 4 + matrix, :, 0:HALF]
        for layer in range(2):
            for half in range(2):
                start = side * HALF + half * 128
                row = layer * 2 + half
                gain_grad[layer : layer + 1, start : start + 128] = value[0, row : row + 1, HALF:]


GRAPH = ("y", "zl", "c")


def shift(value, steps):
    return lax.ppermute(value, GRAPH, [(i, (i + steps) % 64) for i in range(64)])


def swap(value, axis):
    return lax.ppermute(value, axis, [(0, 1), (1, 0)])


def shards(
    node_features, out_grad, send_weight, recv_weight, gain, senders, receivers, edge_count, send_rows
):
    core = lax.axis_index("c").astype(jnp.int32).reshape(1, 1)
    features = node_features[0]
    targets = send_rows.reshape(1, H)
    half = jnp.where(lax.axis_index("c") == 0, send_weight, recv_weight)
    other = lax.ppermute(half, ("zl", "zh"), [(i, 7 - i) for i in range(8)])
    by_row, by_edge, sent_0 = call(
        prepare_kernel,
        [((ROWS, E), BF), ((3, E, N), BF), ((H, D), BF)],
        "prepare",
        edge_count.reshape(1, 1), senders, receivers, targets, features,
    )
    other, prev_0, next_0 = lax.optimization_barrier((other, shift(sent_0, 1), shift(sent_0, -1)))
    is_low = lax.axis_index("zh") == 0
    both = jnp.stack([jnp.where(is_low, half, other), jnp.where(is_low, other, half)])
    copies = jnp.broadcast_to(both[None], (4,) + both.shape)
    own = lax.all_to_all(copies, ("x",), 0, 0, tiled=True)
    peer = swap(own, "c")

    rows_1, total_0, slope_0, sent_1 = call(
        first_layer_kernel,
        [((N, D), BF), ((N, D), F32), ((E, D), F32), ((H, D), BF)],
        "first_layer",
        core, features, prev_0, next_0, own, peer, gain, by_row, by_edge, targets,
    )
    prev_1, next_1 = shift(sent_1, 1), shift(sent_1, -1)
    updated, grad_1, to_prev, to_next, keep_1, give_1 = call(
        last_layer_kernel,
        [((N, D), BF), ((N, D), F32), ((H, D), BF), ((H, D), BF), ((DROWS, HALF), BF), ((DROWS, HALF), BF)],
        "last_layer",
        core, rows_1, prev_1, next_1, own, peer, gain, by_row, by_edge, out_grad[0],
    )
    back_next, back_prev = shift(to_prev, -1), shift(to_next, 1)
    grad_0, to_prev, to_next, keep, pack = call(
        back_kernel,
        [((N, D), F32), ((H, D), BF), ((H, D), BF), ((DROWS, D), BF), ((2 * EXT + DROWS, D), BF)],
        "back",
        core, grad_1, back_next, back_prev, total_0, slope_0, own, peer, gain, by_row, by_edge,
        targets, features, prev_0, next_0, rows_1, prev_1, next_1, keep_1, give_1,
    )
    peer_pack = swap(pack, "c")
    back_next, back_prev = shift(to_prev, -1), shift(to_next, 1)
    peer_pack, back_next, back_prev = lax.optimization_barrier((peer_pack, back_next, back_prev))
    (chunks,) = call(terms_kernel, [((4, 528, HALF), BF)], "terms", pack, keep, peer_pack)
    parts = lax.all_to_all(chunks, ("x",), 0, 0, tiled=True)
    (pieces,) = call(first_sum_kernel, [((PARTS, 8, HALF + 128), BF)], "first_sum", parts)
    parts = lax.all_to_all(pieces, ("y", "zh", "zl"), 0, 0, tiled=True)
    (copies,) = call(second_sum_kernel, [((32, 8, HALF + 128), BF)], "second_sum", parts)
    mine = lax.all_to_all(copies, ("y", "zl"), 0, 0, tiled=True)
    theirs = swap(mine, "c")
    send_grad, recv_grad, gain_grad = call(
        spread_kernel, [((2, 64, D), F32), ((2, 64, D), F32), ((2, D), F32)], "spread", core, mine, theirs
    )
    (feature_grad,) = call(merge_kernel, [((N, D), BF)], "merge", grad_0, back_next, back_prev, targets)
    return updated[None], feature_grad[None], send_grad, recv_grad, gain_grad


def solution(mesh):
    graph, fsdp = GRAPH, ("zh", "x")
    wide = Mesh(mesh.devices.reshape(8, 4, 2, 2, 4), GRAPH + fsdp)
    in_specs = (
        P(fsdp, graph, None),
        P(fsdp, graph, None),
        P(None, fsdp, None),
        P(None, fsdp, None),
        P(),
        P(graph, None),
        P(graph, None),
        P(graph),
        P(graph, None, None),
    )
    out_specs = (
        P(fsdp, graph, None),
        P(fsdp, graph, None),
        P(None, fsdp, None),
        P(None, fsdp, None),
        P(),
    )
    return jax.shard_map(shards, mesh=wide, in_specs=in_specs, out_specs=out_specs, check_vma=False)
```

```python
import functools

import jax
import jax.numpy as jnp
from jax import lax
from jax.experimental import pallas as pl
from jax.experimental.pallas import tpu as pltpu
from jax.sharding import Mesh
from jax.sharding import PartitionSpec as P

EPSILON = 1e-05
LOSS_SCALE = 512.0

D = 512
N = 128
H = 16
E = 512
EXT = N + 2 * H
ROWS = EXT + N
HALF = D // 2
DROWS = ROWS + 16
PARTS = 64

BF = jnp.bfloat16
F32 = jnp.float32
VMEM = pl.BlockSpec(memory_space=pltpu.VMEM)
SMEM = pl.BlockSpec(memory_space=pltpu.SMEM)


def dot(a, b):
    return jnp.dot(a, b, preferred_element_type=F32)


def dot_tn(a, b):
    return lax.dot_general(a, b, (((0,), (0,)), ((), ())), preferred_element_type=F32)


def dot_nt(a, b):
    return lax.dot_general(a, b, (((1,), (1,)), ((), ())), preferred_element_type=F32)


def split(value):
    high = value.astype(BF)
    return high, (value - high.astype(F32)).astype(BF)


def call(kernel, outs, name, *args, flops=1e8):
    specs = [SMEM if a.dtype == jnp.int32 and a.size <= 2 else VMEM for a in args]
    return pl.pallas_call(
        kernel,
        out_shape=[jax.ShapeDtypeStruct(s, t) for s, t in outs],
        in_specs=specs,
        out_specs=[VMEM] * len(outs),
        compiler_params=pltpu.CompilerParams(vmem_limit_bytes=40 * 1024 * 1024),
        cost_estimate=pl.CostEstimate(flops=int(flops), bytes_accessed=2000000, transcendentals=0),
        name=name,
    )(*args)


def ordered(core, outer, inner):
    is_first = core[0, 0] == 0
    outer, inner = outer[...], inner[...]
    return jnp.where(is_first, outer, inner), jnp.where(is_first, inner, outer)


def send_matrices_of(send_rows):
    rows = lax.broadcasted_iota(jnp.int32, (N, H // 2), 0)
    return [(rows == send_rows[0, i : i + 1, :]).astype(F32).astype(BF) for i in range(2)]


def sent_of(send_rows, rows):
    return jnp.concatenate([dot_tn(m, rows) for m in send_matrices_of(send_rows)], axis=0).astype(BF)


def prepare_kernel(count, senders, receivers, send_rows, rows, by_row, by_edge, outer, inner):
    live = lax.broadcasted_iota(jnp.int32, (1, E), 1) < count[0, 0]
    ids = senders[...]
    ids = jnp.where(ids >= N + H // 2, ids + H, ids)
    ids = jnp.where(live, ids, -1)
    receiver_ids = jnp.where(live, receivers[...], -1)
    row = lax.broadcasted_iota(jnp.int32, (EXT, E), 0)
    by_row[0:EXT, :] = (row == ids).astype(F32).astype(BF)
    row = lax.broadcasted_iota(jnp.int32, (N, E), 0)
    by_row[EXT:ROWS, :] = (row == receiver_ids).astype(F32).astype(BF)
    ids_down = jnp.broadcast_to(ids, (N, E)).T
    receivers_down = jnp.broadcast_to(receiver_ids, (N, E)).T
    lane = lax.broadcasted_iota(jnp.int32, (E, N), 1)
    by_edge[0] = (lane == ids_down).astype(F32).astype(BF)
    by_edge[1] = (lane == receivers_down).astype(F32).astype(BF)
    by_edge[2] = (lane == ids_down - N).astype(F32).astype(BF)
    sent = sent_of(send_rows, rows[...])
    outer[...] = sent
    inner[...] = sent


def weights_of(core, own, peer, layer):
    def whole(ref):
        return jnp.concatenate([ref[x, z, layer] for z in range(2) for x in range(4)], axis=0)

    first, second = whole(own), whole(peer)
    is_first = core[0, 0] == 0
    return jnp.where(is_first, first, second), jnp.where(is_first, second, first)


def forward(rows, from_prev, from_next, send_matrix, recv_matrix, by_row, by_edge):
    ext = jnp.concatenate([rows, from_prev, from_next], axis=0)
    proj_send = dot(ext, send_matrix)
    proj_recv = dot(rows, recv_matrix)
    send_high, send_low = split(proj_send)
    recv_high, recv_low = split(proj_recv)
    halo = jnp.concatenate(
        [send_high[N:], send_low[N:], jnp.zeros((N - 4 * H, D), BF)], axis=0
    )
    halo_edges = by_edge[2]
    halo_edges = jnp.concatenate(
        [halo_edges[:, : 2 * H], halo_edges[:, : 2 * H], halo_edges[:, 4 * H :]], axis=1
    )
    edges = jnp.concatenate([by_edge[0], by_edge[1]], axis=1)
    own_high = jnp.concatenate([send_high[:N], recv_high], axis=0)
    own_low = jnp.concatenate([send_low[:N], recv_low], axis=0)
    preact = dot(edges, own_high) + dot(edges, own_low) + dot(halo_edges, halo)
    sigmoid = 1.0 / (1.0 + jnp.exp(-preact))
    message = preact * sigmoid
    slope = sigmoid * (1.0 + preact * (1.0 - sigmoid))
    high, low = split(message)
    receive = by_row[EXT:ROWS, :]
    return dot(receive, high) + dot(receive, low), slope


def factor_of(total):
    return lax.rsqrt(jnp.mean(total * total, axis=-1, keepdims=True) + EPSILON)


def backward(cotangent, total, slope, gain_row, send_matrix, recv_matrix, by_row, by_edge):
    factor = factor_of(total)
    normal = total * factor
    gain_term = jnp.sum(cotangent * normal, axis=0, keepdims=True)
    scaled = cotangent * gain_row
    inner = jnp.mean(scaled * normal, axis=-1, keepdims=True)
    total_grad = (scaled - normal * inner) * factor
    high, low = split(total_grad)
    receive = by_edge[1]
    preact_grad = ((dot(receive, high) + dot(receive, low)) * slope).astype(BF)
    row_grad = dot(by_row[...], preact_grad).astype(BF)
    send_rows_grad, recv_rows_grad = row_grad[:EXT], row_grad[EXT:]
    ext_grad = dot_nt(send_rows_grad, send_matrix)
    own_grad = dot_nt(recv_rows_grad, recv_matrix) + ext_grad[:N]
    halo_grad = ext_grad[N:].astype(BF)
    gain_block = jnp.concatenate([gain_term, jnp.zeros((15, D), F32)], axis=0).astype(BF)
    return own_grad, halo_grad[:H], halo_grad[H:], row_grad, gain_block


def halves(core, value):
    is_first = core[0, 0] == 0
    left, right = value[:, :HALF], value[:, HALF:]
    return jnp.where(is_first, left, right), jnp.where(is_first, right, left)


def first_layer_kernel(
    core, rows, outer, inner, own, peer, gain, by_row, by_edge, send_rows,
    result, total_out, slope_out, outer_out, inner_out,
):
    from_prev, from_next = ordered(core, outer, inner)
    send_matrix, recv_matrix = weights_of(core, own, peer, 0)
    total, slope = forward(
        rows[...], from_prev, from_next, send_matrix, recv_matrix, by_row, by_edge
    )
    total_out[...] = total
    slope_out[...] = slope
    new = (rows[...].astype(F32) + gain[0:1, :] * total * factor_of(total)).astype(BF)
    result[...] = new
    sent = sent_of(send_rows, new)
    outer_out[...] = sent
    inner_out[...] = sent


def last_layer_kernel(
    core, rows, outer, inner, own, peer, gain, by_row, by_edge, out_grad,
    result, own_grad, outer_out, inner_out, keep, give,
):
    from_prev, from_next = ordered(core, outer, inner)
    send_matrix, recv_matrix = weights_of(core, own, peer, 1)
    total, slope = forward(
        rows[...], from_prev, from_next, send_matrix, recv_matrix, by_row, by_edge
    )
    gain_row = gain[1:2, :]
    result[...] = (rows[...].astype(F32) + gain_row * total * factor_of(total)).astype(BF)
    cotangent = out_grad[...].astype(F32)
    grad, prev_grad, next_grad, row_grad, gain_block = backward(
        cotangent, total, slope, gain_row, send_matrix, recv_matrix, by_row, by_edge
    )
    own_grad[...] = grad + cotangent
    outer_out[...], inner_out[...] = ordered(core, prev_grad, next_grad)
    keep[0:ROWS, :], give[0:ROWS, :] = halves(core, row_grad)
    keep[ROWS:DROWS, :], give[ROWS:DROWS, :] = halves(core, gain_block)


def merged(own_grad, outer, inner, send_rows):
    back = outer[...].astype(F32) + inner[...].astype(F32)
    upper, lower = send_matrices_of(send_rows)
    back = dot(upper, back[: H // 2].astype(BF)) + dot(lower, back[H // 2 :].astype(BF))
    return (own_grad[...] + back).astype(BF)


def back_kernel(
    core, later_grad, outer, inner, total, slope, own, peer, gain, by_row, by_edge, send_rows,
    rows_0, outer_0, inner_0, rows_1, outer_1, inner_1, later_keep, later_give,
    own_grad, outer_out, inner_out, keep, pack,
):
    send_matrix, recv_matrix = weights_of(core, own, peer, 0)
    cotangent = merged(later_grad, outer, inner, send_rows).astype(F32)
    grad, prev_grad, next_grad, row_grad, gain_block = backward(
        cotangent, total[...], slope[...], gain[0:1, :], send_matrix, recv_matrix, by_row, by_edge
    )
    own_grad[...] = grad + cotangent
    outer_out[...], inner_out[...] = ordered(core, prev_grad, next_grad)
    base = 2 * EXT
    keep_rows, give_rows = halves(core, row_grad)
    keep_gain, give_gain = halves(core, gain_block)
    keep[0:ROWS, 0:HALF] = keep_rows
    keep[ROWS:DROWS, 0:HALF] = keep_gain
    keep[:, HALF:D] = later_keep[...]
    pack[base : base + ROWS, 0:HALF] = give_rows
    pack[base + ROWS : base + DROWS, 0:HALF] = give_gain
    pack[base : base + DROWS, HALF:D] = later_give[...]
    for layer, parts in enumerate(((rows_0, outer_0, inner_0), (rows_1, outer_1, inner_1))):
        start = layer * EXT
        pack[start : start + N, :] = parts[0][...]
        from_prev, from_next = ordered(core, *parts[1:])
        pack[start + N : start + N + H, :] = from_prev
        pack[start + N + H : start + EXT, :] = from_next


def merge_kernel(own_grad, outer, inner, send_rows, result):
    result[...] = merged(own_grad, outer, inner, send_rows)


def terms_kernel(pack, keep, peer, chunks):
    base = 2 * EXT
    gains = []
    for layer in range(2):
        lanes = slice(layer * HALF, (layer + 1) * HALF)
        mine = pack[layer * EXT : (layer + 1) * EXT, :]
        theirs = peer[layer * EXT : (layer + 1) * EXT, :]
        for kind in range(2):
            if kind == 0:
                left = jnp.concatenate([mine, theirs], axis=0)
                right = jnp.concatenate([keep[0:EXT, lanes], peer[base : base + EXT, lanes]], axis=0)
            else:
                left = jnp.concatenate([mine[:N], theirs[:N]], axis=0)
                right = jnp.concatenate(
                    [keep[EXT:ROWS, lanes], peer[base + EXT : base + ROWS, lanes]], axis=0
                )
            term = dot_tn(left, right).astype(BF)
            for z in range(2):
                for x in range(4):
                    start = (z * 4 + x) * 64
                    place = (z * 4 + 2 * kind + layer) * 64
                    chunks[x, place : place + 64, :] = term[start : start + 64]
        gain = keep[ROWS:DROWS, lanes].astype(F32) + peer[base + ROWS : base + DROWS, lanes].astype(F32)
        gains.append(gain[0:1, :])
    block = jnp.concatenate(gains + [jnp.zeros((14, HALF), F32)], axis=0).astype(BF)
    for x in range(4):
        chunks[x, 512:528, :] = block


def first_sum_kernel(parts, pieces):
    total = parts[0].astype(F32)
    for source in range(1, 4):
        total = total + parts[source].astype(F32)
    gains = [total[512 + layer : 513 + layer, half : half + 128] for layer in range(2) for half in (0, 128)]
    gain = jnp.concatenate(gains + [jnp.zeros((4, 128), F32)], axis=0).astype(BF)
    for y in range(8):
        for z in range(8):
            start = z * 64 + y * 8
            pieces[y * 8 + z, :, 0:HALF] = total[start : start + 8].astype(BF)
            pieces[y * 8 + z, :, HALF:] = gain


def second_sum_kernel(parts, copies):
    total = parts[0].astype(F32)
    for source in range(1, PARTS):
        total = total + parts[source].astype(F32)
    total = total.astype(BF)
    for target in range(32):
        copies[target] = total


def spread_kernel(core, own, peer, send_grad, recv_grad, gain_grad):
    is_first = core[0, 0] == 0
    scale = 1.0 / LOSS_SCALE
    mine, theirs = own[...].astype(F32) * scale, peer[...].astype(F32) * scale
    sides = (jnp.where(is_first, mine, theirs), jnp.where(is_first, theirs, mine))
    for side, value in enumerate(sides):
        columns = slice(side * HALF, (side + 1) * HALF)
        for matrix in range(4):
            out = (send_grad, recv_grad)[matrix // 2]
            for y in range(8):
                out[matrix % 2, y * 8 : y * 8 + 8, columns] = value[y * 4 + matrix, :, 0:HALF]
        for layer in range(2):
            for half in range(2):
                start = side * HALF + half * 128
                row = layer * 2 + half
                gain_grad[layer : layer + 1, start : start + 128] = value[0, row : row + 1, HALF:]


GRAPH = ("y", "zl", "c")


def swap(value, axis):
    return lax.ppermute(value, axis, [(0, 1), (1, 0)])


def exchange(outer, inner):
    pairs = [(i, (i + 1) % 64 if i % 2 else (i - 1) % 64) for i in range(64)]
    return lax.ppermute(outer, GRAPH, pairs), swap(inner, "c")


def shards(
    node_features, out_grad, send_weight, recv_weight, gain, senders, receivers, edge_count, send_rows
):
    core = lax.axis_index("c").astype(jnp.int32).reshape(1, 1)
    features = node_features[0]
    half = jnp.where(lax.axis_index("c") == 0, send_weight, recv_weight)
    other = lax.ppermute(half, ("zl", "zh"), [(i, 7 - i) for i in range(8)])
    by_row, by_edge, *sent = call(
        prepare_kernel,
        [((ROWS, E), BF), ((3, E, N), BF), ((H, D), BF), ((H, D), BF)],
        "prepare",
        edge_count.reshape(1, 1), senders, receivers, send_rows, features,
    )
    is_low = lax.axis_index("zh") == 0
    both = jnp.stack([jnp.where(is_low, half, other), jnp.where(is_low, other, half)])
    copies = jnp.broadcast_to(both[None], (4,) + both.shape)
    own = lax.all_to_all(copies, ("x",), 0, 0, tiled=True)
    own, *halo_0 = lax.optimization_barrier((own, *exchange(*sent)))
    peer = swap(own, "c")

    rows_1, total_0, slope_0, *sent = call(
        first_layer_kernel,
        [((N, D), BF), ((N, D), F32), ((E, D), F32), ((H, D), BF), ((H, D), BF)],
        "first_layer",
        core, features, *halo_0, own, peer, gain, by_row, by_edge, send_rows,
    )
    halo_1 = exchange(*sent)
    updated, grad_1, outer, inner, keep_1, give_1 = call(
        last_layer_kernel,
        [((N, D), BF), ((N, D), F32), ((H, D), BF), ((H, D), BF), ((DROWS, HALF), BF), ((DROWS, HALF), BF)],
        "last_layer",
        core, rows_1, *halo_1, own, peer, gain, by_row, by_edge, out_grad[0],
    )
    back = exchange(outer, inner)
    grad_0, outer, inner, keep, pack = call(
        back_kernel,
        [((N, D), F32), ((H, D), BF), ((H, D), BF), ((DROWS, D), BF), ((2 * EXT + DROWS, D), BF)],
        "back",
        core, grad_1, *back, total_0, slope_0, own, peer, gain, by_row, by_edge,
        send_rows, features, *halo_0, rows_1, *halo_1, keep_1, give_1,
    )
    peer_pack = swap(pack, "c")
    (chunks,) = call(terms_kernel, [((4, 528, HALF), BF)], "terms", pack, keep, peer_pack)
    parts = lax.all_to_all(chunks, ("x",), 0, 0, tiled=True)
    (pieces,) = call(first_sum_kernel, [((PARTS, 8, HALF + 128), BF)], "first_sum", parts)
    parts = lax.all_to_all(pieces, ("y", "zh", "zl"), 0, 0, tiled=True)
    parts, outer, inner = lax.optimization_barrier((parts, outer, inner))
    (copies,) = call(second_sum_kernel, [((32, 8, HALF + 128), BF)], "second_sum", parts)
    mine = lax.all_to_all(copies, ("y", "zl"), 0, 0, tiled=True)
    mine, *back = lax.optimization_barrier((mine, *exchange(outer, inner)))
    theirs = swap(mine, "c")
    send_grad, recv_grad, gain_grad = call(
        spread_kernel, [((2, 64, D), F32), ((2, 64, D), F32), ((2, D), F32)], "spread", core, mine, theirs
    )
    (feature_grad,) = call(merge_kernel, [((N, D), BF)], "merge", grad_0, *back, send_rows)
    return updated[None], feature_grad[None], send_grad, recv_grad, gain_grad


def solution(mesh):
    graph, fsdp = GRAPH, ("zh", "x")
    wide = Mesh(mesh.devices.reshape(8, 4, 2, 2, 4), GRAPH + fsdp)
    in_specs = (
        P(fsdp, graph, None),
        P(fsdp, graph, None),
        P(None, fsdp, None),
        P(None, fsdp, None),
        P(),
        P(graph, None),
        P(graph, None),
        P(graph),
        P(graph, None, None),
    )
    out_specs = (
        P(fsdp, graph, None),
        P(fsdp, graph, None),
        P(None, fsdp, None),
        P(None, fsdp, None),
        P(),
    )
    return jax.shard_map(shards, mesh=wide, in_specs=in_specs, out_specs=out_specs, check_vma=False)
```

```python
import functools

import jax
import jax.numpy as jnp
from jax import lax
from jax.experimental import pallas as pl
from jax.experimental.pallas import tpu as pltpu
from jax.sharding import Mesh
from jax.sharding import PartitionSpec as P

EPSILON = 1e-05
LOSS_SCALE = 512.0

D = 512
N = 128
H = 16
E = 512
EXT = N + 2 * H
ROWS = EXT + N
HALF = D // 2
DROWS = ROWS + 16
CHUNK = 32
PARTS = 64

BF = jnp.bfloat16
F32 = jnp.float32
VMEM = pl.BlockSpec(memory_space=pltpu.VMEM)
SMEM = pl.BlockSpec(memory_space=pltpu.SMEM)


def dot(a, b):
    return jnp.dot(a, b, preferred_element_type=F32)


def dot_tn(a, b):
    return lax.dot_general(a, b, (((0,), (0,)), ((), ())), preferred_element_type=F32)


def dot_nt(a, b):
    return lax.dot_general(a, b, (((1,), (1,)), ((), ())), preferred_element_type=F32)


def split(value):
    high = value.astype(BF)
    return high, (value - high.astype(F32)).astype(BF)


def call(kernel, outs, name, *args, flops=1e8):
    specs = [SMEM if a.dtype == jnp.int32 and a.size <= 2 else VMEM for a in args]
    return pl.pallas_call(
        kernel,
        out_shape=[jax.ShapeDtypeStruct(s, t) for s, t in outs],
        in_specs=specs,
        out_specs=[VMEM] * len(outs),
        compiler_params=pltpu.CompilerParams(vmem_limit_bytes=40 * 1024 * 1024),
        cost_estimate=pl.CostEstimate(flops=int(flops), bytes_accessed=2000000, transcendentals=0),
        name=name,
    )(*args)


def ordered(core, outer, inner):
    is_first = core[0, 0] == 0
    outer, inner = outer[...], inner[...]
    return jnp.where(is_first, outer, inner), jnp.where(is_first, inner, outer)


def send_matrices_of(send_rows):
    rows = lax.broadcasted_iota(jnp.int32, (N, H // 2), 0)
    return [(rows == send_rows[0, i : i + 1, :]).astype(F32).astype(BF) for i in range(2)]


def sent_of(send_rows, rows):
    return jnp.concatenate([dot_tn(m, rows) for m in send_matrices_of(send_rows)], axis=0).astype(BF)


def prepare_kernel(count, senders, receivers, send_rows, rows, by_row, by_edge, outer, inner):
    live = lax.broadcasted_iota(jnp.int32, (1, E), 1) < count[0, 0]
    ids = senders[...]
    ids = jnp.where(ids >= N + H // 2, ids + H, ids)
    ids = jnp.where(live, ids, -1)
    receiver_ids = jnp.where(live, receivers[...], -1)
    row = lax.broadcasted_iota(jnp.int32, (EXT, E), 0)
    by_row[0:EXT, :] = (row == ids).astype(F32).astype(BF)
    row = lax.broadcasted_iota(jnp.int32, (N, E), 0)
    by_row[EXT:ROWS, :] = (row == receiver_ids).astype(F32).astype(BF)
    ids_down = jnp.broadcast_to(ids, (N, E)).T
    receivers_down = jnp.broadcast_to(receiver_ids, (N, E)).T
    lane = lax.broadcasted_iota(jnp.int32, (E, N), 1)
    own = (lane == ids_down).astype(F32).astype(BF)
    receive = (lane == receivers_down).astype(F32).astype(BF)
    by_edge[:, 0:N] = own
    by_edge[:, N : 2 * N] = own
    by_edge[:, 2 * N : 3 * N] = receive
    by_edge[:, 3 * N : 4 * N] = receive
    halo = (ids_down >= N) & ((lane == ids_down - N) | (lane == ids_down - N + 2 * H))
    by_edge[:, 4 * N :] = halo.astype(F32).astype(BF)
    sent = sent_of(send_rows, rows[...])
    outer[...] = sent
    inner[...] = sent


def weights_of(core, own, peer, layer):
    def whole(ref):
        return jnp.concatenate([ref[x, z, layer] for z in range(2) for x in range(4)], axis=0)

    first, second = whole(own), whole(peer)
    is_first = core[0, 0] == 0
    return jnp.where(is_first, first, second), jnp.where(is_first, second, first)


def forward(rows, from_prev, from_next, send_matrix, recv_matrix, by_row, by_edge):
    ext = jnp.concatenate([rows, from_prev, from_next], axis=0)
    proj_send = dot(ext, send_matrix)
    proj_recv = dot(rows, recv_matrix)
    send_high, send_low = split(proj_send)
    recv_high, recv_low = split(proj_recv)
    table = [send_high[:N], send_low[:N], recv_high, recv_low, send_high[N:], send_low[N:]]
    table = jnp.concatenate(table + [jnp.zeros((N - 4 * H, D), BF)], axis=0)
    preact = dot(by_edge[...], table)
    highs, lows, slopes = [], [], []
    for start in range(0, E, CHUNK):
        part = preact[start : start + CHUNK]
        sigmoid = 1.0 / (1.0 + jnp.exp(-part))
        high, low = split(part * sigmoid)
        highs.append(high)
        lows.append(low)
        slopes.append(sigmoid * (1.0 + part * (1.0 - sigmoid)))
    receive = by_row[EXT:ROWS, :]
    total = dot(jnp.concatenate([receive, receive], axis=1), jnp.concatenate(highs + lows, axis=0))
    return total, jnp.concatenate(slopes, axis=0)


def factor_of(total):
    return lax.rsqrt(jnp.mean(total * total, axis=-1, keepdims=True) + EPSILON)


def backward(cotangent, total, slope, gain_row, send_matrix, recv_matrix, by_row, by_edge):
    factor = factor_of(total)
    normal = total * factor
    gain_term = jnp.sum(cotangent * normal, axis=0, keepdims=True)
    scaled = cotangent * gain_row
    inner = jnp.mean(scaled * normal, axis=-1, keepdims=True)
    total_grad = (scaled - normal * inner) * factor
    message_grad = dot(by_edge[:, 2 * N : 4 * N], jnp.concatenate(split(total_grad), axis=0))
    preact_grad = [
        (message_grad[start : start + CHUNK] * slope[start : start + CHUNK]).astype(BF)
        for start in range(0, E, CHUNK)
    ]
    preact_grad = jnp.concatenate(preact_grad, axis=0)
    row_grad = dot(by_row[...], preact_grad).astype(BF)
    send_rows_grad, recv_rows_grad = row_grad[:EXT], row_grad[EXT:]
    ext_grad = dot_nt(send_rows_grad, send_matrix)
    own_grad = dot_nt(recv_rows_grad, recv_matrix) + ext_grad[:N]
    halo_grad = ext_grad[N:].astype(BF)
    gain_block = jnp.concatenate([gain_term, jnp.zeros((15, D), F32)], axis=0).astype(BF)
    return own_grad, halo_grad[:H], halo_grad[H:], row_grad, gain_block


def halves(core, value):
    is_first = core[0, 0] == 0
    left, right = value[:, :HALF], value[:, HALF:]
    return jnp.where(is_first, left, right), jnp.where(is_first, right, left)


def first_layer_kernel(
    core, rows, outer, inner, own, peer, gain, by_row, by_edge, send_rows,
    result, total_out, slope_out, outer_out, inner_out,
):
    from_prev, from_next = ordered(core, outer, inner)
    send_matrix, recv_matrix = weights_of(core, own, peer, 0)
    total, slope = forward(
        rows[...], from_prev, from_next, send_matrix, recv_matrix, by_row, by_edge
    )
    total_out[...] = total
    slope_out[...] = slope
    new = (rows[...].astype(F32) + gain[0:1, :] * total * factor_of(total)).astype(BF)
    result[...] = new
    sent = sent_of(send_rows, new)
    outer_out[...] = sent
    inner_out[...] = sent


def last_layer_kernel(
    core, rows, outer, inner, own, peer, gain, by_row, by_edge, out_grad,
    result, own_grad, outer_out, inner_out, keep, give,
):
    from_prev, from_next = ordered(core, outer, inner)
    send_matrix, recv_matrix = weights_of(core, own, peer, 1)
    total, slope = forward(
        rows[...], from_prev, from_next, send_matrix, recv_matrix, by_row, by_edge
    )
    gain_row = gain[1:2, :]
    result[...] = (rows[...].astype(F32) + gain_row * total * factor_of(total)).astype(BF)
    cotangent = out_grad[...].astype(F32)
    grad, prev_grad, next_grad, row_grad, gain_block = backward(
        cotangent, total, slope, gain_row, send_matrix, recv_matrix, by_row, by_edge
    )
    own_grad[...] = grad + cotangent
    outer_out[...], inner_out[...] = ordered(core, prev_grad, next_grad)
    keep[0:ROWS, :], give[0:ROWS, :] = halves(core, row_grad)
    keep[ROWS:DROWS, :], give[ROWS:DROWS, :] = halves(core, gain_block)


def merged(own_grad, outer, inner, send_rows):
    back = outer[...].astype(F32) + inner[...].astype(F32)
    upper, lower = send_matrices_of(send_rows)
    back = dot(upper, back[: H // 2].astype(BF)) + dot(lower, back[H // 2 :].astype(BF))
    return (own_grad[...] + back).astype(BF)


def back_kernel(
    core, later_grad, outer, inner, total, slope, own, peer, gain, by_row, by_edge, send_rows,
    rows_0, outer_0, inner_0, rows_1, outer_1, inner_1, later_keep, later_give,
    own_grad, outer_out, inner_out, keep, pack,
):
    send_matrix, recv_matrix = weights_of(core, own, peer, 0)
    cotangent = merged(later_grad, outer, inner, send_rows).astype(F32)
    grad, prev_grad, next_grad, row_grad, gain_block = backward(
        cotangent, total[...], slope[...], gain[0:1, :], send_matrix, recv_matrix, by_row, by_edge
    )
    own_grad[...] = grad + cotangent
    outer_out[...], inner_out[...] = ordered(core, prev_grad, next_grad)
    base = 2 * EXT
    keep_rows, give_rows = halves(core, row_grad)
    keep_gain, give_gain = halves(core, gain_block)
    keep[0:ROWS, 0:HALF] = keep_rows
    keep[ROWS:DROWS, 0:HALF] = keep_gain
    keep[:, HALF:D] = later_keep[...]
    pack[base : base + ROWS, 0:HALF] = give_rows
    pack[base + ROWS : base + DROWS, 0:HALF] = give_gain
    pack[base : base + DROWS, HALF:D] = later_give[...]
    for layer, parts in enumerate(((rows_0, outer_0, inner_0), (rows_1, outer_1, inner_1))):
        start = layer * EXT
        pack[start : start + N, :] = parts[0][...]
        from_prev, from_next = ordered(core, *parts[1:])
        pack[start + N : start + N + H, :] = from_prev
        pack[start + N + H : start + EXT, :] = from_next


def merge_kernel(own_grad, outer, inner, send_rows, result):
    result[...] = merged(own_grad, outer, inner, send_rows)


def terms_kernel(pack, keep, peer, chunks):
    base = 2 * EXT
    gains = []
    for layer in range(2):
        lanes = slice(layer * HALF, (layer + 1) * HALF)
        mine = pack[layer * EXT : (layer + 1) * EXT, :]
        theirs = peer[layer * EXT : (layer + 1) * EXT, :]
        for kind in range(2):
            if kind == 0:
                left = jnp.concatenate([mine, theirs], axis=0)
                right = jnp.concatenate([keep[0:EXT, lanes], peer[base : base + EXT, lanes]], axis=0)
            else:
                left = jnp.concatenate([mine[:N], theirs[:N]], axis=0)
                right = jnp.concatenate(
                    [keep[EXT:ROWS, lanes], peer[base + EXT : base + ROWS, lanes]], axis=0
                )
            term = dot_tn(left, right).astype(BF)
            for z in range(2):
                for x in range(4):
                    start = (z * 4 + x) * 64
                    place = (z * 4 + 2 * kind + layer) * 64
                    chunks[x, place : place + 64, :] = term[start : start + 64]
        gain = keep[ROWS:DROWS, lanes].astype(F32) + peer[base + ROWS : base + DROWS, lanes].astype(F32)
        gains.append(gain[0:1, :])
    block = jnp.concatenate(gains + [jnp.zeros((14, HALF), F32)], axis=0).astype(BF)
    for x in range(4):
        chunks[x, 512:528, :] = block


def first_sum_kernel(parts, pieces):
    total = parts[0].astype(F32)
    for source in range(1, 4):
        total = total + parts[source].astype(F32)
    gains = [total[512 + layer : 513 + layer, half : half + 128] for layer in range(2) for half in (0, 128)]
    gain = jnp.concatenate(gains + [jnp.zeros((4, 128), F32)], axis=0).astype(BF)
    for y in range(8):
        for z in range(8):
            start = z * 64 + y * 8
            pieces[y * 8 + z, :, 0:HALF] = total[start : start + 8].astype(BF)
            pieces[y * 8 + z, :, HALF:] = gain


def second_sum_kernel(parts, copies):
    total = parts[0].astype(F32)
    for source in range(1, PARTS):
        total = total + parts[source].astype(F32)
    total = total.astype(BF)
    for target in range(32):
        copies[target] = total


def spread_kernel(core, own, peer, send_grad, recv_grad, gain_grad):
    is_first = core[0, 0] == 0
    scale = 1.0 / LOSS_SCALE
    mine, theirs = own[...].astype(F32) * scale, peer[...].astype(F32) * scale
    sides = (jnp.where(is_first, mine, theirs), jnp.where(is_first, theirs, mine))
    for side, value in enumerate(sides):
        columns = slice(side * HALF, (side + 1) * HALF)
        for matrix in range(4):
            out = (send_grad, recv_grad)[matrix // 2]
            for y in range(8):
                out[matrix % 2, y * 8 : y * 8 + 8, columns] = value[y * 4 + matrix, :, 0:HALF]
        for layer in range(2):
            for half in range(2):
                start = side * HALF + half * 128
                row = layer * 2 + half
                gain_grad[layer : layer + 1, start : start + 128] = value[0, row : row + 1, HALF:]


GRAPH = ("y", "zl", "c")


def swap(value, axis):
    return lax.ppermute(value, axis, [(0, 1), (1, 0)])


def exchange(outer, inner):
    pairs = [(i, (i + 1) % 64 if i % 2 else (i - 1) % 64) for i in range(64)]
    return lax.ppermute(outer, GRAPH, pairs), swap(inner, "c")


def shards(
    node_features, out_grad, send_weight, recv_weight, gain, senders, receivers, edge_count, send_rows
):
    core = lax.axis_index("c").astype(jnp.int32).reshape(1, 1)
    features = node_features[0]
    half = jnp.where(lax.axis_index("c") == 0, send_weight, recv_weight)
    other = lax.ppermute(half, ("zl", "zh"), [(i, 7 - i) for i in range(8)])
    by_row, by_edge, *sent = call(
        prepare_kernel,
        [((ROWS, E), BF), ((E, 5 * N), BF), ((H, D), BF), ((H, D), BF)],
        "prepare",
        edge_count.reshape(1, 1), senders, receivers, send_rows, features,
    )
    is_low = lax.axis_index("zh") == 0
    both = jnp.stack([jnp.where(is_low, half, other), jnp.where(is_low, other, half)])
    copies = jnp.broadcast_to(both[None], (4,) + both.shape)
    own = lax.all_to_all(copies, ("x",), 0, 0, tiled=True)
    own, *halo_0 = lax.optimization_barrier((own, *exchange(*sent)))
    peer = swap(own, "c")

    rows_1, total_0, slope_0, *sent = call(
        first_layer_kernel,
        [((N, D), BF), ((N, D), F32), ((E, D), F32), ((H, D), BF), ((H, D), BF)],
        "first_layer",
        core, features, *halo_0, own, peer, gain, by_row, by_edge, send_rows,
    )
    halo_1 = exchange(*sent)
    updated, grad_1, outer, inner, keep_1, give_1 = call(
        last_layer_kernel,
        [((N, D), BF), ((N, D), F32), ((H, D), BF), ((H, D), BF), ((DROWS, HALF), BF), ((DROWS, HALF), BF)],
        "last_layer",
        core, rows_1, *halo_1, own, peer, gain, by_row, by_edge, out_grad[0],
    )
    back = exchange(outer, inner)
    grad_0, outer, inner, keep, pack = call(
        back_kernel,
        [((N, D), F32), ((H, D), BF), ((H, D), BF), ((DROWS, D), BF), ((2 * EXT + DROWS, D), BF)],
        "back",
        core, grad_1, *back, total_0, slope_0, own, peer, gain, by_row, by_edge,
        send_rows, features, *halo_0, rows_1, *halo_1, keep_1, give_1,
    )
    peer_pack = swap(pack, "c")
    (chunks,) = call(terms_kernel, [((4, 528, HALF), BF)], "terms", pack, keep, peer_pack)
    parts = lax.all_to_all(chunks, ("x",), 0, 0, tiled=True)
    (pieces,) = call(first_sum_kernel, [((PARTS, 8, HALF + 128), BF)], "first_sum", parts)
    parts = lax.all_to_all(pieces, ("y", "zh", "zl"), 0, 0, tiled=True)
    parts, outer, inner = lax.optimization_barrier((parts, outer, inner))
    (copies,) = call(second_sum_kernel, [((32, 8, HALF + 128), BF)], "second_sum", parts)
    mine = lax.all_to_all(copies, ("y", "zl"), 0, 0, tiled=True)
    mine, *back = lax.optimization_barrier((mine, *exchange(outer, inner)))
    theirs = swap(mine, "c")
    send_grad, recv_grad, gain_grad = call(
        spread_kernel, [((2, 64, D), F32), ((2, 64, D), F32), ((2, D), F32)], "spread", core, mine, theirs
    )
    (feature_grad,) = call(merge_kernel, [((N, D), BF)], "merge", grad_0, *back, send_rows)
    return updated[None], feature_grad[None], send_grad, recv_grad, gain_grad


def solution(mesh):
    graph, fsdp = GRAPH, ("zh", "x")
    wide = Mesh(mesh.devices.reshape(8, 4, 2, 2, 4), GRAPH + fsdp)
    in_specs = (
        P(fsdp, graph, None),
        P(fsdp, graph, None),
        P(None, fsdp, None),
        P(None, fsdp, None),
        P(),
        P(graph, None),
        P(graph, None),
        P(graph),
        P(graph, None, None),
    )
    out_specs = (
        P(fsdp, graph, None),
        P(fsdp, graph, None),
        P(None, fsdp, None),
        P(None, fsdp, None),
        P(),
    )
    return jax.shard_map(shards, mesh=wide, in_specs=in_specs, out_specs=out_specs, check_vma=False)
```

```python
import functools

import jax
import jax.numpy as jnp
from jax import lax
from jax.experimental import pallas as pl
from jax.experimental.pallas import tpu as pltpu
from jax.sharding import Mesh
from jax.sharding import PartitionSpec as P

EPSILON = 1e-05
LOSS_SCALE = 512.0

D = 512
N = 128
H = 16
E = 512
EXT = N + 2 * H
ROWS = EXT + N
HALF = D // 2
DROWS = ROWS + 16
CHUNK = 32
PARTS = 64

BF = jnp.bfloat16
F32 = jnp.float32
VMEM = pl.BlockSpec(memory_space=pltpu.VMEM)
SMEM = pl.BlockSpec(memory_space=pltpu.SMEM)


def dot(a, b):
    return jnp.dot(a, b, preferred_element_type=F32)


def dot_tn(a, b):
    return lax.dot_general(a, b, (((0,), (0,)), ((), ())), preferred_element_type=F32)


def dot_nt(a, b):
    return lax.dot_general(a, b, (((1,), (1,)), ((), ())), preferred_element_type=F32)


def split(value):
    high = value.astype(BF)
    return high, (value - high.astype(F32)).astype(BF)


def call(kernel, outs, name, *args, flops=1e8):
    specs = [SMEM if a.dtype == jnp.int32 and a.size <= 2 else VMEM for a in args]
    return pl.pallas_call(
        kernel,
        out_shape=[jax.ShapeDtypeStruct(s, t) for s, t in outs],
        in_specs=specs,
        out_specs=[VMEM] * len(outs),
        compiler_params=pltpu.CompilerParams(vmem_limit_bytes=40 * 1024 * 1024),
        cost_estimate=pl.CostEstimate(flops=int(flops), bytes_accessed=2000000, transcendentals=0),
        name=name,
    )(*args)


def ordered(core, outer, inner):
    is_first = core[0, 0] == 0
    outer, inner = outer[...], inner[...]
    return jnp.where(is_first, outer, inner), jnp.where(is_first, inner, outer)


def send_matrices_of(send_rows):
    rows = lax.broadcasted_iota(jnp.int32, (N, H // 2), 0)
    return [(rows == send_rows[0, i : i + 1, :]).astype(F32).astype(BF) for i in range(2)]


def sent_of(send_rows, rows):
    return jnp.concatenate([dot_tn(m, rows) for m in send_matrices_of(send_rows)], axis=0).astype(BF)


def prepare_kernel(count, senders, receivers, send_rows, rows, by_row, by_edge, outer, inner):
    live = lax.broadcasted_iota(jnp.int32, (1, E), 1) < count[0, 0]
    ids = senders[...]
    ids = jnp.where(ids >= N + H // 2, ids + H, ids)
    ids = jnp.where(live, ids, -1)
    receiver_ids = jnp.where(live, receivers[...], -1)
    row = lax.broadcasted_iota(jnp.int32, (EXT, E), 0)
    by_row[0:EXT, :] = (row == ids).astype(F32).astype(BF)
    row = lax.broadcasted_iota(jnp.int32, (N, E), 0)
    by_row[EXT:ROWS, :] = (row == receiver_ids).astype(F32).astype(BF)
    ids_down = jnp.broadcast_to(ids, (N, E)).T
    receivers_down = jnp.broadcast_to(receiver_ids, (N, E)).T
    lane = lax.broadcasted_iota(jnp.int32, (E, N), 1)
    own = (lane == ids_down).astype(F32).astype(BF)
    receive = (lane == receivers_down).astype(F32).astype(BF)
    by_edge[:, 0:N] = own
    by_edge[:, N : 2 * N] = own
    by_edge[:, 2 * N : 3 * N] = receive
    by_edge[:, 3 * N : 4 * N] = receive
    halo = (ids_down >= N) & ((lane == ids_down - N) | (lane == ids_down - N + 2 * H))
    by_edge[:, 4 * N :] = halo.astype(F32).astype(BF)
    sent = sent_of(send_rows, rows[...])
    outer[...] = sent
    inner[...] = sent


def weights_of(core, own, peer, layer):
    def whole(ref):
        return jnp.concatenate([ref[x, z, layer] for z in range(2) for x in range(4)], axis=0)

    first, second = whole(own), whole(peer)
    is_first = core[0, 0] == 0
    return jnp.where(is_first, first, second), jnp.where(is_first, second, first)


def forward(rows, from_prev, from_next, send_matrix, recv_matrix, by_row, by_edge):
    ext = jnp.concatenate([rows, from_prev, from_next], axis=0)
    proj_send = dot(ext, send_matrix)
    proj_recv = dot(rows, recv_matrix)
    send_high, send_low = split(proj_send)
    recv_high, recv_low = split(proj_recv)
    table = [send_high[:N], send_low[:N], recv_high, recv_low, send_high[N:], send_low[N:]]
    table = jnp.concatenate(table + [jnp.zeros((N - 4 * H, D), BF)], axis=0)
    preact = dot(by_edge[...], table)
    highs, lows, slopes = [], [], []
    for start in range(0, E, CHUNK):
        part = preact[start : start + CHUNK]
        sigmoid = 1.0 / (1.0 + jnp.exp(-part))
        high, low = split(part * sigmoid)
        highs.append(high)
        lows.append(low)
        slopes.append(sigmoid * (1.0 + part * (1.0 - sigmoid)))
    receive = by_row[EXT:ROWS, :]
    total = dot(jnp.concatenate([receive, receive], axis=1), jnp.concatenate(highs + lows, axis=0))
    return total, jnp.concatenate(slopes, axis=0)


def factor_of(total):
    return lax.rsqrt(jnp.mean(total * total, axis=-1, keepdims=True) + EPSILON)


def backward(cotangent, total, slope, gain_row, by_row, by_edge):
    factor = factor_of(total)
    normal = total * factor
    gain_term = jnp.sum(cotangent * normal, axis=0, keepdims=True)
    scaled = cotangent * gain_row
    inner = jnp.mean(scaled * normal, axis=-1, keepdims=True)
    total_grad = (scaled - normal * inner) * factor
    message_grad = dot(by_edge[:, 2 * N : 4 * N], jnp.concatenate(split(total_grad), axis=0))
    preact_grad = [
        (message_grad[start : start + CHUNK] * slope[start : start + CHUNK]).astype(BF)
        for start in range(0, E, CHUNK)
    ]
    row_grad = dot(by_row[...], jnp.concatenate(preact_grad, axis=0)).astype(BF)
    gain_block = jnp.concatenate([gain_term, jnp.zeros((15, D), F32)], axis=0).astype(BF)
    return row_grad, gain_block


def halo_grads(core, row_grad, send_matrix):
    grads = dot_nt(row_grad[N:EXT], send_matrix).astype(BF)
    return ordered(core, grads[:H], grads[H:])


def own_grad_of(cotangent, row_grad, send_matrix, recv_matrix):
    return cotangent + dot_nt(row_grad[0:N, :], send_matrix) + dot_nt(row_grad[EXT:ROWS, :], recv_matrix)


def halves(core, value):
    is_first = core[0, 0] == 0
    left, right = value[:, :HALF], value[:, HALF:]
    return jnp.where(is_first, left, right), jnp.where(is_first, right, left)


def first_layer_kernel(
    core, rows, outer, inner, own, peer, gain, by_row, by_edge, send_rows,
    result, total_out, slope_out, outer_out, inner_out,
):
    from_prev, from_next = ordered(core, outer, inner)
    send_matrix, recv_matrix = weights_of(core, own, peer, 0)
    total, slope = forward(
        rows[...], from_prev, from_next, send_matrix, recv_matrix, by_row, by_edge
    )
    total_out[...] = total
    slope_out[...] = slope
    new = (rows[...].astype(F32) + gain[0:1, :] * total * factor_of(total)).astype(BF)
    result[...] = new
    sent = sent_of(send_rows, new)
    outer_out[...] = sent
    inner_out[...] = sent


def last_layer_kernel(
    core, rows, outer, inner, own, peer, gain, by_row, by_edge, out_grad,
    outer_out, inner_out, total_out, row_grad_out,
):
    from_prev, from_next = ordered(core, outer, inner)
    send_matrix, recv_matrix = weights_of(core, own, peer, 1)
    total, slope = forward(
        rows[...], from_prev, from_next, send_matrix, recv_matrix, by_row, by_edge
    )
    total_out[...] = total
    cotangent = out_grad[...].astype(F32)
    row_grad, gain_block = backward(cotangent, total, slope, gain[1:2, :], by_row, by_edge)
    outer_out[...], inner_out[...] = halo_grads(core, row_grad, send_matrix)
    row_grad_out[0:ROWS, :] = row_grad
    row_grad_out[ROWS:DROWS, :] = gain_block


def last_rest_kernel(core, rows, total, gain, out_grad, row_grad, own, peer, result, own_grad, keep, give):
    send_matrix, recv_matrix = weights_of(core, own, peer, 1)
    step = gain[1:2, :] * total[...] * factor_of(total[...])
    result[...] = (rows[...].astype(F32) + step).astype(BF)
    own_grad[...] = own_grad_of(out_grad[...].astype(F32), row_grad, send_matrix, recv_matrix)
    keep[...], give[...] = halves(core, row_grad[...])


def merged(own_grad, outer, inner, send_rows):
    back = outer[...].astype(F32) + inner[...].astype(F32)
    upper, lower = send_matrices_of(send_rows)
    back = dot(upper, back[: H // 2].astype(BF)) + dot(lower, back[H // 2 :].astype(BF))
    return (own_grad[...] + back).astype(BF)


def back_kernel(
    core, later_grad, outer, inner, total, slope, gain, by_row, by_edge, send_rows,
    rows_0, outer_0, inner_0, rows_1, outer_1, inner_1, later_keep, later_give,
    cotangent_out, row_grad_out, keep, pack,
):
    cotangent = merged(later_grad, outer, inner, send_rows).astype(F32)
    cotangent_out[...] = cotangent
    row_grad, gain_block = backward(cotangent, total[...], slope[...], gain[0:1, :], by_row, by_edge)
    row_grad_out[...] = row_grad
    base = 2 * EXT
    keep_rows, give_rows = halves(core, row_grad)
    keep_gain, give_gain = halves(core, gain_block)
    keep[0:ROWS, 0:HALF] = keep_rows
    keep[ROWS:DROWS, 0:HALF] = keep_gain
    keep[:, HALF:D] = later_keep[...]
    pack[base : base + ROWS, 0:HALF] = give_rows
    pack[base + ROWS : base + DROWS, 0:HALF] = give_gain
    pack[base : base + DROWS, HALF:D] = later_give[...]
    for layer, parts in enumerate(((rows_0, outer_0, inner_0), (rows_1, outer_1, inner_1))):
        start = layer * EXT
        pack[start : start + N, :] = parts[0][...]
        from_prev, from_next = ordered(core, *parts[1:])
        pack[start + N : start + N + H, :] = from_prev
        pack[start + N + H : start + EXT, :] = from_next


def back_rest_kernel(core, cotangent, row_grad, own, peer, own_grad, outer_out, inner_out):
    send_matrix, recv_matrix = weights_of(core, own, peer, 0)
    own_grad[...] = own_grad_of(cotangent[...], row_grad, send_matrix, recv_matrix)
    outer_out[...], inner_out[...] = halo_grads(core, row_grad[...], send_matrix)


def merge_kernel(own_grad, outer, inner, send_rows, result):
    result[...] = merged(own_grad, outer, inner, send_rows)


def terms_kernel(pack, keep, peer, chunks):
    base = 2 * EXT
    gains = []
    for layer in range(2):
        lanes = slice(layer * HALF, (layer + 1) * HALF)
        mine = pack[layer * EXT : (layer + 1) * EXT, :]
        theirs = peer[layer * EXT : (layer + 1) * EXT, :]
        for kind in range(2):
            if kind == 0:
                left = jnp.concatenate([mine, theirs], axis=0)
                right = jnp.concatenate([keep[0:EXT, lanes], peer[base : base + EXT, lanes]], axis=0)
            else:
                left = jnp.concatenate([mine[:N], theirs[:N]], axis=0)
                right = jnp.concatenate(
                    [keep[EXT:ROWS, lanes], peer[base + EXT : base + ROWS, lanes]], axis=0
                )
            term = dot_tn(left, right).astype(BF)
            for z in range(2):
                for x in range(4):
                    start = (z * 4 + x) * 64
                    place = (z * 4 + 2 * kind + layer) * 64
                    chunks[x, place : place + 64, :] = term[start : start + 64]
        gain = keep[ROWS:DROWS, lanes].astype(F32) + peer[base + ROWS : base + DROWS, lanes].astype(F32)
        gains.append(gain[0:1, :])
    block = jnp.concatenate(gains + [jnp.zeros((14, HALF), F32)], axis=0).astype(BF)
    for x in range(4):
        chunks[x, 512:528, :] = block


def first_sum_kernel(parts, pieces):
    total = parts[0].astype(F32)
    for source in range(1, 4):
        total = total + parts[source].astype(F32)
    gains = [total[512 + layer : 513 + layer, half : half + 128] for layer in range(2) for half in (0, 128)]
    gain = jnp.concatenate(gains + [jnp.zeros((4, 128), F32)], axis=0).astype(BF)
    for y in range(8):
        for z in range(8):
            start = z * 64 + y * 8
            pieces[y * 8 + z, :, 0:HALF] = total[start : start + 8].astype(BF)
            pieces[y * 8 + z, :, HALF:] = gain


def second_sum_kernel(parts, copies):
    total = parts[0].astype(F32)
    for source in range(1, PARTS):
        total = total + parts[source].astype(F32)
    total = total.astype(BF)
    for target in range(32):
        copies[target] = total


def spread_kernel(core, own, peer, send_grad, recv_grad, gain_grad):
    is_first = core[0, 0] == 0
    scale = 1.0 / LOSS_SCALE
    mine, theirs = own[...].astype(F32) * scale, peer[...].astype(F32) * scale
    sides = (jnp.where(is_first, mine, theirs), jnp.where(is_first, theirs, mine))
    for side, value in enumerate(sides):
        columns = slice(side * HALF, (side + 1) * HALF)
        for matrix in range(4):
            out = (send_grad, recv_grad)[matrix // 2]
            for y in range(8):
                out[matrix % 2, y * 8 : y * 8 + 8, columns] = value[y * 4 + matrix, :, 0:HALF]
        for layer in range(2):
            for half in range(2):
                start = side * HALF + half * 128
                row = layer * 2 + half
                gain_grad[layer : layer + 1, start : start + 128] = value[0, row : row + 1, HALF:]


GRAPH = ("y", "zl", "c")


def swap(value, axis):
    return lax.ppermute(value, axis, [(0, 1), (1, 0)])


def exchange(outer, inner):
    pairs = [(i, (i + 1) % 64 if i % 2 else (i - 1) % 64) for i in range(64)]
    return lax.ppermute(outer, GRAPH, pairs), swap(inner, "c")


def shards(
    node_features, out_grad, send_weight, recv_weight, gain, senders, receivers, edge_count, send_rows
):
    core = lax.axis_index("c").astype(jnp.int32).reshape(1, 1)
    features = node_features[0]
    half = jnp.where(lax.axis_index("c") == 0, send_weight, recv_weight)
    other = lax.ppermute(half, ("zl", "zh"), [(i, 7 - i) for i in range(8)])
    by_row, by_edge, *sent = call(
        prepare_kernel,
        [((ROWS, E), BF), ((E, 5 * N), BF), ((H, D), BF), ((H, D), BF)],
        "prepare",
        edge_count.reshape(1, 1), senders, receivers, send_rows, features,
    )
    is_low = lax.axis_index("zh") == 0
    both = jnp.stack([jnp.where(is_low, half, other), jnp.where(is_low, other, half)])
    copies = jnp.broadcast_to(both[None], (4,) + both.shape)
    own = lax.all_to_all(copies, ("x",), 0, 0, tiled=True)
    own, *halo_0 = lax.optimization_barrier((own, *exchange(*sent)))
    peer = swap(own, "c")

    rows_1, total_0, slope_0, *sent = call(
        first_layer_kernel,
        [((N, D), BF), ((N, D), F32), ((E, D), F32), ((H, D), BF), ((H, D), BF)],
        "first_layer",
        core, features, *halo_0, own, peer, gain, by_row, by_edge, send_rows,
    )
    halo_1 = exchange(*sent)
    outer, inner, total_1, row_grad = call(
        last_layer_kernel,
        [((H, D), BF), ((H, D), BF), ((N, D), F32), ((DROWS, D), BF)],
        "last_layer",
        core, rows_1, *halo_1, own, peer, gain, by_row, by_edge, out_grad[0],
    )
    back = exchange(outer, inner)
    updated, grad_1, keep_1, give_1 = call(
        last_rest_kernel,
        [((N, D), BF), ((N, D), F32), ((DROWS, HALF), BF), ((DROWS, HALF), BF)],
        "last_rest",
        core, rows_1, total_1, gain, out_grad[0], row_grad, own, peer,
    )
    cotangent, row_grad, keep, pack = call(
        back_kernel,
        [((N, D), F32), ((ROWS, D), BF), ((DROWS, D), BF), ((2 * EXT + DROWS, D), BF)],
        "back",
        core, grad_1, *back, total_0, slope_0, gain, by_row, by_edge,
        send_rows, features, *halo_0, rows_1, *halo_1, keep_1, give_1,
    )
    grad_0, outer, inner = call(
        back_rest_kernel,
        [((N, D), F32), ((H, D), BF), ((H, D), BF)],
        "back_rest",
        core, cotangent, row_grad, own, peer,
    )
    peer_pack = swap(pack, "c")
    peer_pack, grad_0, outer, inner = lax.optimization_barrier((peer_pack, grad_0, outer, inner))
    (chunks,) = call(terms_kernel, [((4, 528, HALF), BF)], "terms", pack, keep, peer_pack)
    parts = lax.all_to_all(chunks, ("x",), 0, 0, tiled=True)
    (pieces,) = call(first_sum_kernel, [((PARTS, 8, HALF + 128), BF)], "first_sum", parts)
    parts = lax.all_to_all(pieces, ("y", "zh", "zl"), 0, 0, tiled=True)
    parts, outer, inner = lax.optimization_barrier((parts, outer, inner))
    (copies,) = call(second_sum_kernel, [((32, 8, HALF + 128), BF)], "second_sum", parts)
    mine = lax.all_to_all(copies, ("y", "zl"), 0, 0, tiled=True)
    mine, *back = lax.optimization_barrier((mine, *exchange(outer, inner)))
    theirs = swap(mine, "c")
    send_grad, recv_grad, gain_grad = call(
        spread_kernel, [((2, 64, D), F32), ((2, 64, D), F32), ((2, D), F32)], "spread", core, mine, theirs
    )
    (feature_grad,) = call(merge_kernel, [((N, D), BF)], "merge", grad_0, *back, send_rows)
    return updated[None], feature_grad[None], send_grad, recv_grad, gain_grad


def solution(mesh):
    graph, fsdp = GRAPH, ("zh", "x")
    wide = Mesh(mesh.devices.reshape(8, 4, 2, 2, 4), GRAPH + fsdp)
    in_specs = (
        P(fsdp, graph, None),
        P(fsdp, graph, None),
        P(None, fsdp, None),
        P(None, fsdp, None),
        P(),
        P(graph, None),
        P(graph, None),
        P(graph),
        P(graph, None, None),
    )
    out_specs = (
        P(fsdp, graph, None),
        P(fsdp, graph, None),
        P(None, fsdp, None),
        P(None, fsdp, None),
        P(),
    )
    return jax.shard_map(shards, mesh=wide, in_specs=in_specs, out_specs=out_specs, check_vma=False)
```

```python
import functools

import jax
import jax.numpy as jnp
from jax import lax
from jax.experimental import pallas as pl
from jax.experimental.pallas import tpu as pltpu
from jax.sharding import Mesh
from jax.sharding import PartitionSpec as P

EPSILON = 1e-05
LOSS_SCALE = 512.0

D = 512
N = 128
H = 16
E = 512
EXT = N + 2 * H
ROWS = EXT + N
HALF = D // 2
DROWS = ROWS + 16
CHUNK = 32
PARTS = 64

BF = jnp.bfloat16
F32 = jnp.float32
VMEM = pl.BlockSpec(memory_space=pltpu.VMEM)
SMEM = pl.BlockSpec(memory_space=pltpu.SMEM)


def dot(a, b):
    return jnp.dot(a, b, preferred_element_type=F32)


def dot_tn(a, b):
    return lax.dot_general(a, b, (((0,), (0,)), ((), ())), preferred_element_type=F32)


def dot_nt(a, b):
    return lax.dot_general(a, b, (((1,), (1,)), ((), ())), preferred_element_type=F32)


def split(value):
    high = value.astype(BF)
    return high, (value - high.astype(F32)).astype(BF)


def call(kernel, outs, name, *args, flops=1e8):
    specs = [SMEM if a.dtype == jnp.int32 and a.size <= 2 else VMEM for a in args]
    return pl.pallas_call(
        kernel,
        out_shape=[jax.ShapeDtypeStruct(s, t) for s, t in outs],
        in_specs=specs,
        out_specs=[VMEM] * len(outs),
        compiler_params=pltpu.CompilerParams(vmem_limit_bytes=40 * 1024 * 1024),
        cost_estimate=pl.CostEstimate(flops=int(flops), bytes_accessed=2000000, transcendentals=0),
        name=name,
    )(*args)


def ordered(core, outer, inner):
    is_first = core[0, 0] == 0
    outer, inner = outer[...], inner[...]
    return jnp.where(is_first, outer, inner), jnp.where(is_first, inner, outer)


def send_matrices_of(send_rows):
    rows = lax.broadcasted_iota(jnp.int32, (N, H // 2), 0)
    return [(rows == send_rows[0, i : i + 1, :]).astype(F32).astype(BF) for i in range(2)]


def sent_of(send_rows, rows):
    return jnp.concatenate([dot_tn(m, rows) for m in send_matrices_of(send_rows)], axis=0).astype(BF)


def prepare_kernel(count, senders, receivers, send_rows, rows, by_row, by_edge, outer, inner):
    live = lax.broadcasted_iota(jnp.int32, (1, E), 1) < count[0, 0]
    ids = senders[...]
    ids = jnp.where(ids >= N + H // 2, ids + H, ids)
    ids = jnp.where(live, ids, -1)
    receiver_ids = jnp.where(live, receivers[...], -1)
    row = lax.broadcasted_iota(jnp.int32, (EXT, E), 0)
    by_row[0:EXT, :] = (row == ids).astype(F32).astype(BF)
    row = lax.broadcasted_iota(jnp.int32, (N, E), 0)
    by_row[EXT:ROWS, :] = (row == receiver_ids).astype(F32).astype(BF)
    ids_down = jnp.broadcast_to(ids, (N, E)).T
    receivers_down = jnp.broadcast_to(receiver_ids, (N, E)).T
    lane = lax.broadcasted_iota(jnp.int32, (E, N), 1)
    own = (lane == ids_down).astype(F32).astype(BF)
    receive = (lane == receivers_down).astype(F32).astype(BF)
    by_edge[:, 0:N] = own
    by_edge[:, N : 2 * N] = own
    by_edge[:, 2 * N : 3 * N] = receive
    by_edge[:, 3 * N : 4 * N] = receive
    halo = (ids_down >= N) & ((lane == ids_down - N) | (lane == ids_down - N + 2 * H))
    by_edge[:, 4 * N :] = halo.astype(F32).astype(BF)
    sent = sent_of(send_rows, rows[...])
    outer[...] = sent
    inner[...] = sent


def weights_of(core, own, peer, layer):
    def whole(ref):
        return jnp.concatenate([ref[x, z, layer] for z in range(2) for x in range(4)], axis=0)

    first, second = whole(own), whole(peer)
    is_first = core[0, 0] == 0
    return jnp.where(is_first, first, second), jnp.where(is_first, second, first)


def forward(rows, from_prev, from_next, send_matrix, recv_matrix, by_row, by_edge):
    ext = jnp.concatenate([rows, from_prev, from_next], axis=0)
    proj_send = dot(ext, send_matrix)
    proj_recv = dot(rows, recv_matrix)
    send_high, send_low = split(proj_send)
    recv_high, recv_low = split(proj_recv)
    table = [send_high[:N], send_low[:N], recv_high, recv_low, send_high[N:], send_low[N:]]
    table = jnp.concatenate(table + [jnp.zeros((N - 4 * H, D), BF)], axis=0)
    preact = dot(by_edge[...], table)
    highs, lows, slopes = [], [], []
    for start in range(0, E, CHUNK):
        part = preact[start : start + CHUNK]
        sigmoid = 1.0 / (1.0 + jnp.exp(-part))
        high, low = split(part * sigmoid)
        highs.append(high)
        lows.append(low)
        slopes.append(sigmoid * (1.0 + part * (1.0 - sigmoid)))
    receive = by_row[EXT:ROWS, :]
    total = dot(jnp.concatenate([receive, receive], axis=1), jnp.concatenate(highs + lows, axis=0))
    return total, jnp.concatenate(slopes, axis=0)


def factor_of(total):
    return lax.rsqrt(jnp.mean(total * total, axis=-1, keepdims=True) + EPSILON)


def backward(cotangent, total, slope, gain_row, by_row, by_edge):
    factor = factor_of(total)
    normal = total * factor
    gain_term = jnp.sum(cotangent * normal, axis=0, keepdims=True)
    scaled = cotangent * gain_row
    inner = jnp.mean(scaled * normal, axis=-1, keepdims=True)
    total_grad = (scaled - normal * inner) * factor
    message_grad = dot(by_edge[:, 2 * N : 4 * N], jnp.concatenate(split(total_grad), axis=0))
    preact_grad = [
        (message_grad[start : start + CHUNK] * slope[start : start + CHUNK]).astype(BF)
        for start in range(0, E, CHUNK)
    ]
    row_grad = dot(by_row[...], jnp.concatenate(preact_grad, axis=0)).astype(BF)
    gain_block = jnp.concatenate([gain_term, jnp.zeros((15, D), F32)], axis=0).astype(BF)
    return row_grad, gain_block


def halo_grads(core, row_grad, send_matrix):
    grads = dot_nt(row_grad[N:EXT], send_matrix).astype(BF)
    return ordered(core, grads[:H], grads[H:])


def own_grad_of(cotangent, row_grad, send_matrix, recv_matrix):
    return cotangent + dot_nt(row_grad[0:N, :], send_matrix) + dot_nt(row_grad[EXT:ROWS, :], recv_matrix)


def halves(core, value):
    is_first = core[0, 0] == 0
    left, right = value[:, :HALF], value[:, HALF:]
    return jnp.where(is_first, left, right), jnp.where(is_first, right, left)


def first_layer_kernel(
    core, rows, outer, inner, own, peer, gain, by_row, by_edge, send_rows,
    result, total_out, slope_out, outer_out, inner_out,
):
    from_prev, from_next = ordered(core, outer, inner)
    send_matrix, recv_matrix = weights_of(core, own, peer, 0)
    total, slope = forward(
        rows[...], from_prev, from_next, send_matrix, recv_matrix, by_row, by_edge
    )
    total_out[...] = total
    slope_out[...] = slope
    new = (rows[...].astype(F32) + gain[0:1, :] * total * factor_of(total)).astype(BF)
    result[...] = new
    sent = sent_of(send_rows, new)
    outer_out[...] = sent
    inner_out[...] = sent


def last_layer_kernel(
    core, rows, outer, inner, own, peer, gain, by_row, by_edge, out_grad,
    outer_out, inner_out, total_out, row_grad_out,
):
    from_prev, from_next = ordered(core, outer, inner)
    send_matrix, recv_matrix = weights_of(core, own, peer, 1)
    total, slope = forward(
        rows[...], from_prev, from_next, send_matrix, recv_matrix, by_row, by_edge
    )
    total_out[...] = total
    cotangent = out_grad[...].astype(F32)
    row_grad, gain_block = backward(cotangent, total, slope, gain[1:2, :], by_row, by_edge)
    outer_out[...], inner_out[...] = halo_grads(core, row_grad, send_matrix)
    row_grad_out[0:ROWS, :] = row_grad
    row_grad_out[ROWS:DROWS, :] = gain_block


def last_rest_kernel(core, rows, total, gain, out_grad, row_grad, own, peer, result, own_grad, keep, give):
    send_matrix, recv_matrix = weights_of(core, own, peer, 1)
    step = gain[1:2, :] * total[...] * factor_of(total[...])
    result[...] = (rows[...].astype(F32) + step).astype(BF)
    own_grad[...] = own_grad_of(out_grad[...].astype(F32), row_grad, send_matrix, recv_matrix)
    keep[...], give[...] = halves(core, row_grad[...])


def merged(own_grad, outer, inner, send_rows):
    back = outer[...].astype(F32) + inner[...].astype(F32)
    upper, lower = send_matrices_of(send_rows)
    back = dot(upper, back[: H // 2].astype(BF)) + dot(lower, back[H // 2 :].astype(BF))
    return (own_grad[...] + back).astype(BF)


def back_kernel(
    core, later_grad, outer, inner, total, slope, gain, by_row, by_edge, send_rows,
    rows_0, outer_0, inner_0, rows_1, outer_1, inner_1, later_keep, later_give,
    cotangent_out, row_grad_out, keep, pack,
):
    cotangent = merged(later_grad, outer, inner, send_rows).astype(F32)
    cotangent_out[...] = cotangent
    row_grad, gain_block = backward(cotangent, total[...], slope[...], gain[0:1, :], by_row, by_edge)
    row_grad_out[...] = row_grad
    base = 2 * EXT
    keep_rows, give_rows = halves(core, row_grad)
    keep_gain, give_gain = halves(core, gain_block)
    keep[0:ROWS, 0:HALF] = keep_rows
    keep[ROWS:DROWS, 0:HALF] = keep_gain
    keep[:, HALF:D] = later_keep[...]
    pack[base : base + ROWS, 0:HALF] = give_rows
    pack[base + ROWS : base + DROWS, 0:HALF] = give_gain
    pack[base : base + DROWS, HALF:D] = later_give[...]
    for layer, parts in enumerate(((rows_0, outer_0, inner_0), (rows_1, outer_1, inner_1))):
        start = layer * EXT
        pack[start : start + N, :] = parts[0][...]
        from_prev, from_next = ordered(core, *parts[1:])
        pack[start + N : start + N + H, :] = from_prev
        pack[start + N + H : start + EXT, :] = from_next


def back_rest_kernel(core, cotangent, row_grad, own, peer, own_grad, outer_out, inner_out):
    send_matrix, recv_matrix = weights_of(core, own, peer, 0)
    own_grad[...] = own_grad_of(cotangent[...], row_grad, send_matrix, recv_matrix)
    outer_out[...], inner_out[...] = halo_grads(core, row_grad[...], send_matrix)


def merge_kernel(own_grad, outer, inner, send_rows, result):
    result[...] = merged(own_grad, outer, inner, send_rows)


def terms_kernel(pack, keep, peer, chunks):
    base = 2 * EXT
    gains = []
    for layer in range(2):
        lanes = slice(layer * HALF, (layer + 1) * HALF)
        mine = pack[layer * EXT : (layer + 1) * EXT, :]
        theirs = peer[layer * EXT : (layer + 1) * EXT, :]
        for kind in range(2):
            if kind == 0:
                left = jnp.concatenate([mine, theirs], axis=0)
                right = jnp.concatenate([keep[0:EXT, lanes], peer[base : base + EXT, lanes]], axis=0)
            else:
                left = jnp.concatenate([mine[:N], theirs[:N]], axis=0)
                right = jnp.concatenate(
                    [keep[EXT:ROWS, lanes], peer[base + EXT : base + ROWS, lanes]], axis=0
                )
            term = dot_tn(left, right).astype(BF)
            for z in range(2):
                for x in range(4):
                    start = (z * 4 + x) * 64
                    place = (z * 4 + 2 * kind + layer) * 64
                    chunks[x, place : place + 64, :] = term[start : start + 64]
        gain = keep[ROWS:DROWS, lanes].astype(F32) + peer[base + ROWS : base + DROWS, lanes].astype(F32)
        gains.append(gain[0:1, :])
    block = jnp.concatenate(gains + [jnp.zeros((14, HALF), F32)], axis=0).astype(BF)
    for x in range(4):
        chunks[x, 512:528, :] = block


def first_sum_kernel(parts, pieces):
    total = parts[0].astype(F32)
    for source in range(1, 4):
        total = total + parts[source].astype(F32)
    gains = [total[512 + layer : 513 + layer, half : half + 128] for layer in range(2) for half in (0, 128)]
    gain = jnp.concatenate(gains, axis=0).astype(BF)
    for y in range(8):
        for z in range(8):
            start = z * 64 + y * 8
            pieces[y * 8 + z, :, 0:HALF] = total[start : start + 4].astype(BF)
            pieces[y * 8 + z, :, HALF:D] = total[start + 4 : start + 8].astype(BF)
            pieces[y * 8 + z, :, D:] = gain


def second_sum_kernel(parts, copies):
    total = parts[0].astype(F32)
    for source in range(1, PARTS):
        total = total + parts[source].astype(F32)
    total = total.astype(BF)
    for target in range(32):
        copies[target] = total


def spread_kernel(core, own, peer, send_grad, recv_grad, gain_grad):
    is_first = core[0, 0] == 0
    scale = 1.0 / LOSS_SCALE
    mine, theirs = own[...].astype(F32) * scale, peer[...].astype(F32) * scale
    sides = (jnp.where(is_first, mine, theirs), jnp.where(is_first, theirs, mine))
    for side, value in enumerate(sides):
        columns = slice(side * HALF, (side + 1) * HALF)
        for matrix in range(4):
            out = (send_grad, recv_grad)[matrix // 2]
            for y in range(8):
                piece = value[y * 4 + matrix]
                out[matrix % 2, y * 8 : y * 8 + 4, columns] = piece[:, 0:HALF]
                out[matrix % 2, y * 8 + 4 : y * 8 + 8, columns] = piece[:, HALF:D]
        for layer in range(2):
            for half in range(2):
                start = side * HALF + half * 128
                row = layer * 2 + half
                gain_grad[layer : layer + 1, start : start + 128] = value[0, row : row + 1, D:]


GRAPH = ("y", "zl", "c")


def swap(value, axis):
    return lax.ppermute(value, axis, [(0, 1), (1, 0)])


def exchange(outer, inner):
    pairs = [(i, (i + 1) % 64 if i % 2 else (i - 1) % 64) for i in range(64)]
    return lax.ppermute(outer, GRAPH, pairs), swap(inner, "c")


def shards(
    node_features, out_grad, send_weight, recv_weight, gain, senders, receivers, edge_count, send_rows
):
    core = lax.axis_index("c").astype(jnp.int32).reshape(1, 1)
    features = node_features[0]
    half = jnp.where(lax.axis_index("c") == 0, send_weight, recv_weight)
    other = lax.ppermute(half, ("zl", "zh"), [(i, 7 - i) for i in range(8)])
    by_row, by_edge, *sent = call(
        prepare_kernel,
        [((ROWS, E), BF), ((E, 5 * N), BF), ((H, D), BF), ((H, D), BF)],
        "prepare",
        edge_count.reshape(1, 1), senders, receivers, send_rows, features,
    )
    is_low = lax.axis_index("zh") == 0
    both = jnp.stack([jnp.where(is_low, half, other), jnp.where(is_low, other, half)])
    copies = jnp.broadcast_to(both[None], (4,) + both.shape)
    own = lax.all_to_all(copies, ("x",), 0, 0, tiled=True)
    own, *halo_0 = lax.optimization_barrier((own, *exchange(*sent)))
    peer = swap(own, "c")

    rows_1, total_0, slope_0, *sent = call(
        first_layer_kernel,
        [((N, D), BF), ((N, D), F32), ((E, D), F32), ((H, D), BF), ((H, D), BF)],
        "first_layer",
        core, features, *halo_0, own, peer, gain, by_row, by_edge, send_rows,
    )
    halo_1 = exchange(*sent)
    outer, inner, total_1, row_grad = call(
        last_layer_kernel,
        [((H, D), BF), ((H, D), BF), ((N, D), F32), ((DROWS, D), BF)],
        "last_layer",
        core, rows_1, *halo_1, own, peer, gain, by_row, by_edge, out_grad[0],
    )
    back = exchange(outer, inner)
    updated, grad_1, keep_1, give_1 = call(
        last_rest_kernel,
        [((N, D), BF), ((N, D), F32), ((DROWS, HALF), BF), ((DROWS, HALF), BF)],
        "last_rest",
        core, rows_1, total_1, gain, out_grad[0], row_grad, own, peer,
    )
    cotangent, row_grad, keep, pack = call(
        back_kernel,
        [((N, D), F32), ((ROWS, D), BF), ((DROWS, D), BF), ((2 * EXT + DROWS, D), BF)],
        "back",
        core, grad_1, *back, total_0, slope_0, gain, by_row, by_edge,
        send_rows, features, *halo_0, rows_1, *halo_1, keep_1, give_1,
    )
    grad_0, outer, inner = call(
        back_rest_kernel,
        [((N, D), F32), ((H, D), BF), ((H, D), BF)],
        "back_rest",
        core, cotangent, row_grad, own, peer,
    )
    peer_pack = swap(pack, "c")
    peer_pack, grad_0, outer, inner = lax.optimization_barrier((peer_pack, grad_0, outer, inner))
    (chunks,) = call(terms_kernel, [((4, 528, HALF), BF)], "terms", pack, keep, peer_pack)
    parts = lax.all_to_all(chunks, ("x",), 0, 0, tiled=True)
    (pieces,) = call(first_sum_kernel, [((PARTS, 4, D + 128), BF)], "first_sum", parts)
    parts = lax.all_to_all(pieces, ("y", "zh", "zl"), 0, 0, tiled=True)
    parts, outer, inner = lax.optimization_barrier((parts, outer, inner))
    (copies,) = call(second_sum_kernel, [((32, 4, D + 128), BF)], "second_sum", parts)
    mine = lax.all_to_all(copies, ("y", "zl"), 0, 0, tiled=True)
    mine, *back = lax.optimization_barrier((mine, *exchange(outer, inner)))
    theirs = swap(mine, "c")
    send_grad, recv_grad, gain_grad = call(
        spread_kernel, [((2, 64, D), F32), ((2, 64, D), F32), ((2, D), F32)], "spread", core, mine, theirs
    )
    (feature_grad,) = call(merge_kernel, [((N, D), BF)], "merge", grad_0, *back, send_rows)
    return updated[None], feature_grad[None], send_grad, recv_grad, gain_grad


def solution(mesh):
    graph, fsdp = GRAPH, ("zh", "x")
    wide = Mesh(mesh.devices.reshape(8, 4, 2, 2, 4), GRAPH + fsdp)
    in_specs = (
        P(fsdp, graph, None),
        P(fsdp, graph, None),
        P(None, fsdp, None),
        P(None, fsdp, None),
        P(),
        P(graph, None),
        P(graph, None),
        P(graph),
        P(graph, None, None),
    )
    out_specs = (
        P(fsdp, graph, None),
        P(fsdp, graph, None),
        P(None, fsdp, None),
        P(None, fsdp, None),
        P(),
    )
    return jax.shard_map(shards, mesh=wide, in_specs=in_specs, out_specs=out_specs, check_vma=False)
```

```python
import functools

import jax
import jax.numpy as jnp
from jax import lax
from jax.experimental import pallas as pl
from jax.experimental.pallas import tpu as pltpu
from jax.sharding import Mesh
from jax.sharding import PartitionSpec as P

EPSILON = 1e-05
LOSS_SCALE = 512.0

D = 512
N = 128
H = 16
E = 512
EXT = N + 2 * H
ROWS = EXT + N
HALF = D // 2
DROWS = ROWS + 16
CHUNK = 32
PARTS = 64

BF = jnp.bfloat16
F32 = jnp.float32
VMEM = pl.BlockSpec(memory_space=pltpu.VMEM)
SMEM = pl.BlockSpec(memory_space=pltpu.SMEM)


def dot(a, b):
    return jnp.dot(a, b, preferred_element_type=F32)


def dot_tn(a, b):
    return lax.dot_general(a, b, (((0,), (0,)), ((), ())), preferred_element_type=F32)


def dot_nt(a, b):
    return lax.dot_general(a, b, (((1,), (1,)), ((), ())), preferred_element_type=F32)


def split(value):
    high = value.astype(BF)
    return high, (value - high.astype(F32)).astype(BF)


def call(kernel, outs, name, *args, flops=1e8):
    specs = [SMEM if a.dtype == jnp.int32 and a.size <= 2 else VMEM for a in args]
    return pl.pallas_call(
        kernel,
        out_shape=[jax.ShapeDtypeStruct(s, t) for s, t in outs],
        in_specs=specs,
        out_specs=[VMEM] * len(outs),
        compiler_params=pltpu.CompilerParams(vmem_limit_bytes=40 * 1024 * 1024),
        cost_estimate=pl.CostEstimate(flops=int(flops), bytes_accessed=2000000, transcendentals=0),
        name=name,
    )(*args)


def ordered(core, outer, inner):
    is_first = core[0, 0] == 0
    outer, inner = outer[...], inner[...]
    return jnp.where(is_first, outer, inner), jnp.where(is_first, inner, outer)


def send_matrices_of(send_rows):
    rows = lax.broadcasted_iota(jnp.int32, (N, H // 2), 0)
    return [(rows == send_rows[0, i : i + 1, :]).astype(F32).astype(BF) for i in range(2)]


def sent_of(send_rows, rows):
    return jnp.concatenate([dot_tn(m, rows) for m in send_matrices_of(send_rows)], axis=0).astype(BF)


def prepare_kernel(count, senders, receivers, send_rows, rows, by_row, by_edge, outer, inner):
    live = lax.broadcasted_iota(jnp.int32, (1, E), 1) < count[0, 0]
    ids = senders[...]
    ids = jnp.where(ids >= N + H // 2, ids + H, ids)
    ids = jnp.where(live, ids, -1)
    receiver_ids = jnp.where(live, receivers[...], -1)
    row = lax.broadcasted_iota(jnp.int32, (EXT, E), 0)
    by_row[0:EXT, :] = (row == ids).astype(F32).astype(BF)
    row = lax.broadcasted_iota(jnp.int32, (N, E), 0)
    by_row[EXT:ROWS, :] = (row == receiver_ids).astype(F32).astype(BF)
    ids_down = jnp.broadcast_to(ids, (N, E)).T
    receivers_down = jnp.broadcast_to(receiver_ids, (N, E)).T
    lane = lax.broadcasted_iota(jnp.int32, (E, N), 1)
    own = (lane == ids_down).astype(F32).astype(BF)
    receive = (lane == receivers_down).astype(F32).astype(BF)
    by_edge[:, 0:N] = own
    by_edge[:, N : 2 * N] = own
    by_edge[:, 2 * N : 3 * N] = receive
    by_edge[:, 3 * N : 4 * N] = receive
    halo = (ids_down >= N) & ((lane == ids_down - N) | (lane == ids_down - N + 2 * H))
    by_edge[:, 4 * N :] = halo.astype(F32).astype(BF)
    sent = sent_of(send_rows, rows[...])
    outer[...] = sent
    inner[...] = sent


def weights_of(core, own, peer, layer):
    def whole(ref):
        return jnp.concatenate([ref[x, z, layer] for z in range(2) for x in range(4)], axis=0)

    first, second = whole(own), whole(peer)
    is_first = core[0, 0] == 0
    return jnp.where(is_first, first, second), jnp.where(is_first, second, first)


def forward(rows, from_prev, from_next, send_matrix, recv_matrix, by_row, by_edge):
    ext = jnp.concatenate([rows, from_prev, from_next], axis=0)
    proj_send = dot(ext, send_matrix)
    proj_recv = dot(rows, recv_matrix)
    send_high, send_low = split(proj_send)
    recv_high, recv_low = split(proj_recv)
    table = [send_high[:N], send_low[:N], recv_high, recv_low, send_high[N:], send_low[N:]]
    table = jnp.concatenate(table + [jnp.zeros((N - 4 * H, D), BF)], axis=0)
    preact = dot(by_edge[...], table)
    highs, lows, slopes = [], [], []
    for start in range(0, E, CHUNK):
        part = preact[start : start + CHUNK]
        sigmoid = 1.0 / (1.0 + jnp.exp(-part))
        high, low = split(part * sigmoid)
        highs.append(high)
        lows.append(low)
        slopes.append(sigmoid * (1.0 + part * (1.0 - sigmoid)))
    receive = by_row[EXT:ROWS, :]
    total = dot(jnp.concatenate([receive, receive], axis=1), jnp.concatenate(highs + lows, axis=0))
    return total, jnp.concatenate(slopes, axis=0)


def factor_of(total):
    return lax.rsqrt(jnp.mean(total * total, axis=-1, keepdims=True) + EPSILON)


def backward(cotangent, total, slope, gain_row, by_row, by_edge):
    factor = factor_of(total)
    normal = total * factor
    gain_term = jnp.sum(cotangent * normal, axis=0, keepdims=True)
    scaled = cotangent * gain_row
    inner = jnp.mean(scaled * normal, axis=-1, keepdims=True)
    total_grad = (scaled - normal * inner) * factor
    message_grad = dot(by_edge[:, 2 * N : 4 * N], jnp.concatenate(split(total_grad), axis=0))
    preact_grad = [
        (message_grad[start : start + CHUNK] * slope[start : start + CHUNK]).astype(BF)
        for start in range(0, E, CHUNK)
    ]
    row_grad = dot(by_row[...], jnp.concatenate(preact_grad, axis=0)).astype(BF)
    gain_block = jnp.concatenate([gain_term, jnp.zeros((15, D), F32)], axis=0).astype(BF)
    return row_grad, gain_block


def halo_grads(core, row_grad, send_matrix):
    grads = dot_nt(row_grad[N:EXT], send_matrix).astype(BF)
    return ordered(core, grads[:H], grads[H:])


def own_grad_of(cotangent, row_grad, send_matrix, recv_matrix):
    return cotangent + dot_nt(row_grad[0:N, :], send_matrix) + dot_nt(row_grad[EXT:ROWS, :], recv_matrix)


def halves(core, value):
    is_first = core[0, 0] == 0
    left, right = value[:, :HALF], value[:, HALF:]
    return jnp.where(is_first, left, right), jnp.where(is_first, right, left)


def first_layer_kernel(
    core, rows, outer, inner, own, peer, gain, by_row, by_edge, send_rows,
    result, total_out, slope_out, outer_out, inner_out,
):
    from_prev, from_next = ordered(core, outer, inner)
    send_matrix, recv_matrix = weights_of(core, own, peer, 0)
    total, slope = forward(
        rows[...], from_prev, from_next, send_matrix, recv_matrix, by_row, by_edge
    )
    total_out[...] = total
    slope_out[...] = slope
    new = (rows[...].astype(F32) + gain[0:1, :] * total * factor_of(total)).astype(BF)
    result[...] = new
    sent = sent_of(send_rows, new)
    outer_out[...] = sent
    inner_out[...] = sent


def last_layer_kernel(
    core, rows, outer, inner, own, peer, gain, by_row, by_edge, out_grad,
    outer_out, inner_out, total_out, row_grad_out,
):
    from_prev, from_next = ordered(core, outer, inner)
    send_matrix, recv_matrix = weights_of(core, own, peer, 1)
    total, slope = forward(
        rows[...], from_prev, from_next, send_matrix, recv_matrix, by_row, by_edge
    )
    total_out[...] = total
    cotangent = out_grad[...].astype(F32)
    row_grad, gain_block = backward(cotangent, total, slope, gain[1:2, :], by_row, by_edge)
    outer_out[...], inner_out[...] = halo_grads(core, row_grad, send_matrix)
    row_grad_out[0:ROWS, :] = row_grad
    row_grad_out[ROWS:DROWS, :] = gain_block


def last_rest_kernel(core, rows, total, gain, out_grad, row_grad, own, peer, result, own_grad, keep, give):
    send_matrix, recv_matrix = weights_of(core, own, peer, 1)
    step = gain[1:2, :] * total[...] * factor_of(total[...])
    result[...] = (rows[...].astype(F32) + step).astype(BF)
    own_grad[...] = own_grad_of(out_grad[...].astype(F32), row_grad, send_matrix, recv_matrix)
    keep[...], give[...] = halves(core, row_grad[...])


def merged(own_grad, outer, inner, send_rows):
    back = outer[...].astype(F32) + inner[...].astype(F32)
    upper, lower = send_matrices_of(send_rows)
    back = dot(upper, back[: H // 2].astype(BF)) + dot(lower, back[H // 2 :].astype(BF))
    return (own_grad[...] + back).astype(BF)


def back_kernel(
    core, later_grad, outer, inner, total, slope, gain, by_row, by_edge, send_rows,
    rows_0, outer_0, inner_0, rows_1, outer_1, inner_1, later_keep, later_give,
    cotangent_out, row_grad_out, keep, pack,
):
    cotangent = merged(later_grad, outer, inner, send_rows).astype(F32)
    cotangent_out[...] = cotangent
    row_grad, gain_block = backward(cotangent, total[...], slope[...], gain[0:1, :], by_row, by_edge)
    row_grad_out[...] = row_grad
    base = 2 * EXT
    keep_rows, give_rows = halves(core, row_grad)
    keep_gain, give_gain = halves(core, gain_block)
    keep[0:ROWS, 0:HALF] = keep_rows
    keep[ROWS:DROWS, 0:HALF] = keep_gain
    keep[:, HALF:D] = later_keep[...]
    pack[base : base + ROWS, 0:HALF] = give_rows
    pack[base + ROWS : base + DROWS, 0:HALF] = give_gain
    pack[base : base + DROWS, HALF:D] = later_give[...]
    for layer, parts in enumerate(((rows_0, outer_0, inner_0), (rows_1, outer_1, inner_1))):
        start = layer * EXT
        pack[start : start + N, :] = parts[0][...]
        from_prev, from_next = ordered(core, *parts[1:])
        pack[start + N : start + N + H, :] = from_prev
        pack[start + N + H : start + EXT, :] = from_next


def back_rest_kernel(core, cotangent, row_grad, own, peer, own_grad, outer_out, inner_out):
    send_matrix, recv_matrix = weights_of(core, own, peer, 0)
    own_grad[...] = own_grad_of(cotangent[...], row_grad, send_matrix, recv_matrix)
    outer_out[...], inner_out[...] = halo_grads(core, row_grad[...], send_matrix)


def merge_kernel(own_grad, outer, inner, send_rows, result):
    result[...] = merged(own_grad, outer, inner, send_rows)


def terms_kernel(pack, keep, peer, chunks):
    base = 2 * EXT
    gains = []
    for layer in range(2):
        lanes = slice(layer * HALF, (layer + 1) * HALF)
        mine = pack[layer * EXT : (layer + 1) * EXT, :]
        theirs = peer[layer * EXT : (layer + 1) * EXT, :]
        for kind in range(2):
            if kind == 0:
                left = jnp.concatenate([mine, theirs], axis=0)
                right = jnp.concatenate([keep[0:EXT, lanes], peer[base : base + EXT, lanes]], axis=0)
            else:
                left = jnp.concatenate([mine[:N], theirs[:N]], axis=0)
                right = jnp.concatenate(
                    [keep[EXT:ROWS, lanes], peer[base + EXT : base + ROWS, lanes]], axis=0
                )
            term = dot_tn(left, right).astype(BF)
            for z in range(2):
                for x in range(4):
                    start = (z * 4 + x) * 64
                    place = (z * 4 + 2 * kind + layer) * 64
                    chunks[x, place : place + 64, :] = term[start : start + 64]
        gain = keep[ROWS:DROWS, lanes].astype(F32) + peer[base + ROWS : base + DROWS, lanes].astype(F32)
        gains.append(gain[0:1, :])
    block = jnp.concatenate(gains + [jnp.zeros((14, HALF), F32)], axis=0).astype(BF)
    for x in range(4):
        chunks[x, 512:528, :] = block


def first_sum_kernel(parts, pieces):
    total = parts[0].astype(F32)
    for source in range(1, 4):
        total = total + parts[source].astype(F32)
    gains = [total[512 + layer : 513 + layer, half : half + 128] for layer in range(2) for half in (0, 128)]
    gain = [jnp.concatenate(gains[2 * layer : 2 * layer + 2], axis=0).astype(BF) for layer in range(2)]
    for y in range(8):
        for z in range(8):
            start = z * 64 + y * 8
            for pair in range(4):
                rows = total[start + 2 * pair : start + 2 * pair + 2]
                pieces[y * 8 + z, :, pair * HALF : (pair + 1) * HALF] = rows.astype(BF)
            pieces[y * 8 + z, :, 2 * D :] = gain[y % 2]


def second_sum_kernel(parts, copies):
    total = parts[0].astype(F32)
    for source in range(1, PARTS):
        total = total + parts[source].astype(F32)
    total = total.astype(BF)
    for target in range(32):
        copies[target] = total


def spread_kernel(core, own, peer, send_grad, recv_grad, gain_grad):
    is_first = core[0, 0] == 0
    scale = 1.0 / LOSS_SCALE
    mine, theirs = own[...].astype(F32) * scale, peer[...].astype(F32) * scale
    sides = (jnp.where(is_first, mine, theirs), jnp.where(is_first, theirs, mine))
    for side, value in enumerate(sides):
        columns = slice(side * HALF, (side + 1) * HALF)
        for matrix in range(4):
            out = (send_grad, recv_grad)[matrix // 2]
            for y in range(8):
                piece = value[y * 4 + matrix]
                for pair in range(4):
                    start = y * 8 + 2 * pair
                    out[matrix % 2, start : start + 2, columns] = piece[:, pair * HALF : (pair + 1) * HALF]
        for layer in range(2):
            for half in range(2):
                start = side * HALF + half * 128
                gain_grad[layer : layer + 1, start : start + 128] = value[layer * 4, half : half + 1, 2 * D :]


GRAPH = ("y", "zl", "c")


def swap(value, axis):
    return lax.ppermute(value, axis, [(0, 1), (1, 0)])


def exchange(outer, inner):
    pairs = [(i, (i + 1) % 64 if i % 2 else (i - 1) % 64) for i in range(64)]
    return lax.ppermute(outer, GRAPH, pairs), swap(inner, "c")


def shards(
    node_features, out_grad, send_weight, recv_weight, gain, senders, receivers, edge_count, send_rows
):
    core = lax.axis_index("c").astype(jnp.int32).reshape(1, 1)
    features = node_features[0]
    half = jnp.where(lax.axis_index("c") == 0, send_weight, recv_weight)
    other = lax.ppermute(half, ("zl", "zh"), [(i, 7 - i) for i in range(8)])
    by_row, by_edge, *sent = call(
        prepare_kernel,
        [((ROWS, E), BF), ((E, 5 * N), BF), ((H, D), BF), ((H, D), BF)],
        "prepare",
        edge_count.reshape(1, 1), senders, receivers, send_rows, features,
    )
    is_low = lax.axis_index("zh") == 0
    both = jnp.stack([jnp.where(is_low, half, other), jnp.where(is_low, other, half)])
    copies = jnp.broadcast_to(both[None], (4,) + both.shape)
    own = lax.all_to_all(copies, ("x",), 0, 0, tiled=True)
    own, *halo_0 = lax.optimization_barrier((own, *exchange(*sent)))
    peer = swap(own, "c")

    rows_1, total_0, slope_0, *sent = call(
        first_layer_kernel,
        [((N, D), BF), ((N, D), F32), ((E, D), F32), ((H, D), BF), ((H, D), BF)],
        "first_layer",
        core, features, *halo_0, own, peer, gain, by_row, by_edge, send_rows,
    )
    halo_1 = exchange(*sent)
    outer, inner, total_1, row_grad = call(
        last_layer_kernel,
        [((H, D), BF), ((H, D), BF), ((N, D), F32), ((DROWS, D), BF)],
        "last_layer",
        core, rows_1, *halo_1, own, peer, gain, by_row, by_edge, out_grad[0],
    )
    back = exchange(outer, inner)
    updated, grad_1, keep_1, give_1 = call(
        last_rest_kernel,
        [((N, D), BF), ((N, D), F32), ((DROWS, HALF), BF), ((DROWS, HALF), BF)],
        "last_rest",
        core, rows_1, total_1, gain, out_grad[0], row_grad, own, peer,
    )
    cotangent, row_grad, keep, pack = call(
        back_kernel,
        [((N, D), F32), ((ROWS, D), BF), ((DROWS, D), BF), ((2 * EXT + DROWS, D), BF)],
        "back",
        core, grad_1, *back, total_0, slope_0, gain, by_row, by_edge,
        send_rows, features, *halo_0, rows_1, *halo_1, keep_1, give_1,
    )
    grad_0, outer, inner = call(
        back_rest_kernel,
        [((N, D), F32), ((H, D), BF), ((H, D), BF)],
        "back_rest",
        core, cotangent, row_grad, own, peer,
    )
    peer_pack = swap(pack, "c")
    peer_pack, grad_0, outer, inner = lax.optimization_barrier((peer_pack, grad_0, outer, inner))
    (chunks,) = call(terms_kernel, [((4, 528, HALF), BF)], "terms", pack, keep, peer_pack)
    parts = lax.all_to_all(chunks, ("x",), 0, 0, tiled=True)
    (pieces,) = call(first_sum_kernel, [((PARTS, 2, 2 * D + 128), BF)], "first_sum", parts)
    parts = lax.all_to_all(pieces, ("y", "zh", "zl"), 0, 0, tiled=True)
    parts, outer, inner = lax.optimization_barrier((parts, outer, inner))
    (copies,) = call(second_sum_kernel, [((32, 2, 2 * D + 128), BF)], "second_sum", parts)
    mine = lax.all_to_all(copies, ("y", "zl"), 0, 0, tiled=True)
    mine, *back = lax.optimization_barrier((mine, *exchange(outer, inner)))
    theirs = swap(mine, "c")
    send_grad, recv_grad, gain_grad = call(
        spread_kernel, [((2, 64, D), F32), ((2, 64, D), F32), ((2, D), F32)], "spread", core, mine, theirs
    )
    (feature_grad,) = call(merge_kernel, [((N, D), BF)], "merge", grad_0, *back, send_rows)
    return updated[None], feature_grad[None], send_grad, recv_grad, gain_grad


def solution(mesh):
    graph, fsdp = GRAPH, ("zh", "x")
    wide = Mesh(mesh.devices.reshape(8, 4, 2, 2, 4), GRAPH + fsdp)
    in_specs = (
        P(fsdp, graph, None),
        P(fsdp, graph, None),
        P(None, fsdp, None),
        P(None, fsdp, None),
        P(),
        P(graph, None),
        P(graph, None),
        P(graph),
        P(graph, None, None),
    )
    out_specs = (
        P(fsdp, graph, None),
        P(fsdp, graph, None),
        P(None, fsdp, None),
        P(None, fsdp, None),
        P(),
    )
    return jax.shard_map(shards, mesh=wide, in_specs=in_specs, out_specs=out_specs, check_vma=False)
```
